256 devices in a mesh: res: 32 (over y, x, z_hi), frame: 8 (over z_lo, core).
Axes of the slice: x: 4, y: 4, z: 8 (z_hi: 2, z_lo: 4; z = z_hi * 4 + z_lo), core: 2. Of those that a mesh axis runs over, the one named last changes fastest.
Arguments:
- activations: bfloat16 [16, 4096, 768], P('frame', 'res'), may hold values from -6 to 6
- contacts: int32 [32, 5], replicated, may hold values from 0 to 1, as said below
- frame_index: int32 [16], replicated, may hold values from 0 to 45, as said below
- spatial_qkv: bfloat16 [768, 2304], replicated, may hold values from -8 to 8
- spatial_out: bfloat16 [768, 768], replicated, may hold values from -0.21875 to 0.21875
- time_qkv: bfloat16 [768, 2304], replicated, may hold values from -8 to 8
- time_out: bfloat16 [768, 768], replicated, may hold values from -0.21875 to 0.21875
Outputs:
- layer_out: bfloat16 [16, 4096, 768], P('frame', 'res')
The draws below stay inside these ranges and needn't reach their ends.
Inputs may be any that keep to these rules, and one draw needn't show every extreme that they name: contacts[b, 2] = 1 for every block; contacts are symmetric, contacts[b, 2 + d] = contacts[b + d, 2 - d]; flags that name a block outside 0 to 31 are 0. Strictly increasing, frame_index[0] = 0, frame_index[15] = 45.
All inputs are finite; a program needn't handle non-finite values.
Results may differ from the reference program's by a relative error of at most 0.025.
Values may be sent and summed in bfloat16 or wider, within the bound.
No kernel may reach another device: no remote copies, remote signals or barrier semaphores. Data moves between devices by JAX's collectives and lax.ppermute only.
A program may use at most 128 MiB of HBM per device.

```python
import math
import jax
import jax.numpy as jnp
from jax import lax

D = 768
HEADS = 12
HEAD = 64
BLK = 128
HALO = 2
FRAMES = 16
NBLK = 32
RES = 4096


def projection_triple(base_key, coupling):
    query_key, keys_key, values_key, strength_key = jax.random.split(base_key, 4)
    spread = D ** (-0.5)
    query = jax.random.normal(query_key, (D, D), jnp.float32) * (2.0 * spread)
    values = jax.random.normal(values_key, (D, D), jnp.float32) * spread
    strength = jnp.exp(jax.random.uniform(strength_key, (HEADS,), jnp.float32) * math.log(16.0)) * coupling
    strength = jnp.repeat(strength, HEAD)
    keys = query * strength[None, :] + jax.random.normal(keys_key, (D, D), jnp.float32) * (2.0 * spread)
    return jnp.concatenate([query, keys, values], axis=1).astype(jnp.bfloat16)


def draw_spatial_qkv(key, part):
    key = jax.random.fold_in(key, 11)
    return projection_triple(key, 0.0)


def draw_time_qkv(key, part):
    key = jax.random.fold_in(key, 12)
    return projection_triple(key, 0.0)


def draw_contacts(key, part):
    key = jax.random.fold_in(key, 13)
    activity_key, pair_key = jax.random.split(key, 2)
    activity = jax.random.randint(activity_key, (NBLK,), 0, 4)
    pair_draws = jax.random.randint(pair_key, (NBLK, HALO), 0, 8)
    partner = jnp.arange(NBLK)[:, None] + jnp.arange(1, HALO + 1)[None, :]
    inside = partner < NBLK
    partner_activity = activity[jnp.minimum(partner, NBLK - 1)]
    linked = jnp.where((pair_draws < activity[:, None] + partner_activity + 1) & inside, 1, 0).astype(jnp.int32)
    columns = []
    for distance in range(HALO, 0, -1):
        columns.append(jnp.concatenate([jnp.zeros((distance,), jnp.int32), linked[:NBLK - distance, distance - 1]]))
    columns.append(jnp.ones((NBLK,), jnp.int32))
    for distance in range(1, HALO + 1):
        columns.append(linked[:, distance - 1])
    return jnp.stack(columns, axis=1)


def draw_frame_index(key, part):
    key = jax.random.fold_in(key, 14)
    strides = jax.random.randint(key, (FRAMES - 1,), 1, 4)
    leading = jnp.concatenate([jnp.zeros((1,), jnp.int32), jnp.cumsum(strides[:-1]).astype(jnp.int32)])
    closing = jnp.full((1,), 3 * FRAMES - 3, jnp.int32)
    return jnp.concatenate([leading, closing]).astype(jnp.int32)


def block_scale(rng, shape, cuts, low, high):
    loudness = 1.0
    for axis_at, blocks in cuts:
        steps = jax.random.uniform(jax.random.fold_in(jax.random.fold_in(rng, 6), axis_at), (blocks,), jnp.float32, low / len(cuts), high / len(cuts))
        loudness = loudness * jnp.repeat(jnp.exp(steps), shape[axis_at] // blocks).reshape((-1,) + (1,) * (len(shape) - 1 - axis_at))
    return loudness


def centred(key, shape, width, reach, shards=(), kind=jnp.bfloat16):
    values = jax.random.normal(key, shape, jnp.float32) * width
    if len(shards) > 0:
        values = block_scale(key, shape, shards, -0.22, 0.18) * values
    return jnp.clip(values, min=-reach, max=reach).astype(kind)


def setup_inputs(seed: int = 0) -> dict:
    seeds = jax.random.split(jax.random.key(seed), 8)
    return {
        "activations": centred(seeds[0], (FRAMES, RES, D), 1.0, 6.0, ((0, 8), (1, 32))),
        "contacts": draw_contacts(jax.random.fold_in(seeds[7], 71), 0),
        "frame_index": draw_frame_index(jax.random.fold_in(seeds[7], 71), 0),
        "spatial_qkv": draw_spatial_qkv(jax.random.fold_in(seeds[7], 71), 0),
        "spatial_out": centred(seeds[4], (D, D), D ** -0.5, 0.21875),
        "time_qkv": draw_time_qkv(jax.random.fold_in(seeds[7], 71), 0),
        "time_out": centred(seeds[6], (D, D), D ** -0.5, 0.21875),
    }


def normalize(values_in):
    widened = values_in.astype(jnp.float32)
    mean_square = lax.optimization_barrier(jnp.mean(widened * widened, axis=-1, keepdims=True))
    return (widened * lax.rsqrt(mean_square + 1e-06)).astype(jnp.bfloat16)

def rotate(entries, positions):
    half_size = HEAD // 2
    frequency = 10000.0 ** (-jnp.arange(half_size, dtype=jnp.float32) / half_size)
    angles = positions.astype(jnp.float32)[:, None] * frequency[None, :]
    cosine = jnp.cos(angles)[:, None, None, :]
    sine = jnp.sin(angles)[:, None, None, :]
    first = entries[..., :half_size]
    second = entries[..., half_size:]
    return jnp.concatenate([first * cosine - second * sine, first * sine + second * cosine], axis=-1)

def softmax_rounded(scores):
    top = lax.optimization_barrier(jnp.max(scores, axis=-1, keepdims=True))
    expo = jnp.exp(scores - top)
    weights = (expo / lax.optimization_barrier(jnp.sum(expo, axis=-1, keepdims=True))).astype(jnp.bfloat16)
    return lax.optimization_barrier(weights).astype(jnp.float32)

def time_attend(query, keys, values):
    score_scale = HEAD ** (-0.5)
    scores = jnp.einsum('frhd,grhd->rhfg', query.astype(jnp.float32), keys.astype(jnp.float32)) * score_scale
    weights = softmax_rounded(scores)
    return jnp.einsum('rhfg,grhd->frhd', weights, values.astype(jnp.float32)).astype(jnp.bfloat16)

def reference(activations, contacts, frame_index, spatial_qkv, spatial_out, time_qkv, time_out):
    frame_count, residues, model_width = activations.shape
    head_count = model_width // HEAD
    block_count = residues // BLK
    score_scale = HEAD ** (-0.5)
    flat = activations.reshape(frame_count * residues, model_width)
    normed = normalize(flat)
    projected = jnp.dot(normed, spatial_qkv, preferred_element_type=jnp.float32).astype(jnp.bfloat16)
    projected = projected.reshape(frame_count, block_count, BLK, 3, head_count, HEAD)

    def spatial_frame(frame_proj):
        query = frame_proj[:, :, 0].astype(jnp.float32)
        keys = frame_proj[:, :, 1].astype(jnp.float32)
        values = frame_proj[:, :, 2].astype(jnp.float32)
        padding = ((HALO, HALO), (0, 0), (0, 0), (0, 0))
        keys_padded = jnp.pad(keys, padding)
        values_padded = jnp.pad(values, padding)
        score_list = []
        for column in range(2 * HALO + 1):
            tile = jnp.einsum('brhd,bshd->bhrs', query, keys_padded[column:column + block_count]) * score_scale
            allowed = contacts[:, column][:, None, None, None] > 0
            score_list.append(jnp.where(allowed, tile, -1e+30))
        weights = softmax_rounded(jnp.concatenate(score_list, axis=-1))
        result = jnp.zeros((block_count, BLK, head_count, HEAD), jnp.float32)
        for column in range(2 * HALO + 1):
            part_weights = weights[..., column * BLK:(column + 1) * BLK]
            result = result + jnp.einsum('bhrs,bshd->brhd', part_weights, values_padded[column:column + block_count])
        return result.astype(jnp.bfloat16)
    spatial_mix = lax.map(spatial_frame, projected).reshape(frame_count * residues, model_width)
    hidden = (flat.astype(jnp.float32) + jnp.dot(spatial_mix, spatial_out, preferred_element_type=jnp.float32)).astype(jnp.bfloat16)
    renormed = normalize(hidden)
    time_projected = jnp.dot(renormed, time_qkv, preferred_element_type=jnp.float32).astype(jnp.bfloat16)
    time_projected = time_projected.reshape(frame_count, residues, 3, head_count, HEAD)
    query = rotate(time_projected[:, :, 0].astype(jnp.float32), frame_index).astype(jnp.bfloat16)
    keys = rotate(time_projected[:, :, 1].astype(jnp.float32), frame_index).astype(jnp.bfloat16)
    values = time_projected[:, :, 2]

    def to_blocks(entries):
        return jnp.transpose(entries.reshape(frame_count, block_count, BLK, head_count, HEAD), (1, 0, 2, 3, 4))

    def time_block(operands):
        return time_attend(operands[0], operands[1], operands[2])
    time_mix = lax.map(time_block, (to_blocks(query), to_blocks(keys), to_blocks(values)))
    time_mix = jnp.transpose(time_mix, (1, 0, 2, 3, 4)).reshape(frame_count * residues, model_width)
    layer_out = hidden.astype(jnp.float32) + jnp.dot(time_mix, time_out, preferred_element_type=jnp.float32)
    return layer_out.astype(jnp.bfloat16).reshape(frame_count, residues, model_width)
```

```python
import functools

import jax
import jax.numpy as jnp
from jax import lax
from jax.experimental import pallas as pl
from jax.experimental.pallas import tpu as pltpu
from jax.sharding import Mesh
from jax.sharding import PartitionSpec as P

HEAD = 64
HALO = 2
PAIR = 2 * HEAD
EXCLUDED = -1e30
LOG2E = 1.4426950408889634
COLUMN = ("half", "chip", "core")


def unit_rows(rows):
    widened = rows.astype(jnp.float32)
    mean_square = jnp.mean(widened * widened, axis=-1, keepdims=True)
    return (widened * lax.rsqrt(mean_square + 1e-06)).astype(jnp.bfloat16)


def dot(left, right):
    return jnp.dot(left, right, preferred_element_type=jnp.float32)


def dot_rows(left, right):
    return lax.dot_general(
        left, right, (((1,), (1,)), ((), ())), preferred_element_type=jnp.float32
    )


def pair_attend(query, keys, values, biases):
    lane = lax.broadcasted_iota(jnp.int32, query.shape, 1)
    parts = []
    for head in range(2):
        inside = (lane >= HEAD) if head else (lane < HEAD)
        own = jnp.where(inside, query, jnp.zeros_like(query))
        scores = dot_rows(own, keys) + biases
        top = jnp.max(scores, axis=-1, keepdims=True)
        expo = jnp.exp2(scores - top)
        total = jnp.sum(expo, axis=-1, keepdims=True)
        parts.append(dot(expo.astype(jnp.bfloat16), values) / total)
    return jnp.where(lane < HEAD, parts[0], parts[1]).astype(jnp.bfloat16)


def spatial_kernel(
    half_ref, bias_ref, kept_ref, other_ref, qkv_ref, out_w_ref, hidden_ref, query, keys, values, mix, base
):
    half = half_ref[0]
    width = query.shape[1]
    block = kept_ref.shape[1]
    for tiles, parity in ((kept_ref, half), (other_ref, 1 - half)):
        for step in range(3):
            tile = tiles[step]
            normed = unit_rows(tile)
            at = pl.ds(pl.multiple_of((2 * step + parity) * block, block), block)
            projected = dot(normed, qkv_ref[:, width:]).astype(jnp.bfloat16)
            keys[at, :] = projected[:, :width]
            values[at, :] = projected[:, width:]
            if step == 1:
                here = pl.ds(pl.multiple_of(parity * block, block), block)
                query[here, :] = (dot(normed, qkv_ref[:, :width]) * (LOG2E / 8.0)).astype(jnp.bfloat16)
                base[here, :] = tile
    biases = jnp.concatenate(
        [jnp.broadcast_to(bias_ref[y : y + 1, :], (block, bias_ref.shape[1])) for y in range(2)], axis=0
    )
    for pair in range(width // PAIR):
        at = slice(pair * PAIR, (pair + 1) * PAIR)
        mix[:, at] = pair_attend(query[:, at], keys[:, at], values[:, at], biases)
    hidden = base[...].astype(jnp.float32) + dot(mix[...], out_w_ref[...])
    hidden_ref[...] = hidden.astype(jnp.bfloat16)


def time_kernel(hidden_ref, cos_ref, sin_ref, qkv_ref, out_w_ref, layer_ref, query, keys, values, mix):
    rows, width = hidden_ref.shape
    frames = cos_ref.shape[0]
    group = rows // frames
    normed = unit_rows(hidden_ref[...])
    cosine = jnp.concatenate(
        [jnp.broadcast_to(cos_ref[f : f + 1, :], (group, PAIR)) for f in range(frames)], axis=0
    )
    sine = jnp.concatenate(
        [jnp.broadcast_to(sin_ref[f : f + 1, :], (group, PAIR)) for f in range(frames)], axis=0
    )
    lane = lax.broadcasted_iota(jnp.int32, (rows, PAIR), 1)
    first = (lane % HEAD) < HEAD // 2

    def rotate(entries):
        entries = entries.astype(jnp.bfloat16).astype(jnp.float32)
        swapped = jnp.where(
            first, pltpu.roll(entries, PAIR - HEAD // 2, 1), pltpu.roll(entries, HEAD // 2, 1)
        )
        return entries * cosine + swapped * sine

    projected = dot(normed, qkv_ref[:, : 2 * width])
    for pair in range(width // PAIR):
        at = slice(pair * PAIR, (pair + 1) * PAIR)
        query[:, at] = (rotate(projected[:, at]) * (LOG2E / 8.0)).astype(jnp.bfloat16)
        keys[:, at] = rotate(projected[:, width + pair * PAIR : width + (pair + 1) * PAIR]).astype(jnp.bfloat16)
    values[...] = dot(normed, qkv_ref[:, 2 * width :]).astype(jnp.bfloat16)
    row = lax.broadcasted_iota(jnp.int32, (rows, rows), 0)
    column = lax.broadcasted_iota(jnp.int32, (rows, rows), 1)
    biases = jnp.where(row % group == column % group, 0.0, EXCLUDED)
    for pair in range(width // PAIR):
        at = slice(pair * PAIR, (pair + 1) * PAIR)
        mix[:, at] = pair_attend(query[:, at], keys[:, at], values[:, at], biases)
    layer = (hidden_ref[...].astype(jnp.float32) + dot(mix[...], out_w_ref[...])).astype(jnp.bfloat16)
    per_half = frames // 2
    for j in range(frames):
        frame = 2 * (j % per_half) + j // per_half
        layer_ref[frame * group : (frame + 1) * group, :] = layer[j * group : (j + 1) * group, :]


def shards(activations, contacts, frame_index, spatial_qkv, spatial_out, time_qkv, time_out):
    frames_dev, block, width = activations.shape
    pairs = lax.axis_size("pair")
    pair = lax.axis_index("pair")
    half = lax.axis_index("half")
    kept = lax.dynamic_index_in_dim(activations, half, 0, keepdims=False)
    given = lax.dynamic_index_in_dim(activations, 1 - half, 0, keepdims=False)
    other = lax.ppermute(given, "half", [(0, 1), (1, 0)])

    def from_neighbours(tile):
        before = lax.ppermute(tile, "pair", [(i, (i + 1) % pairs) for i in range(pairs)])
        after = lax.ppermute(tile, "pair", [((i + 1) % pairs, i) for i in range(pairs)])
        return jnp.stack([before, tile, after])

    kept_tiles = from_neighbours(kept)
    other_tiles = from_neighbours(other)
    flags = lax.dynamic_slice_in_dim(contacts, 2 * pair, 2, 0)
    spread = jnp.stack([jnp.pad(flags[0], (0, 1)), jnp.pad(flags[1], (1, 0))])
    biases = jnp.repeat(jnp.where(spread > 0, 0.0, EXCLUDED).astype(jnp.float32), block, axis=1)
    vmem = pl.BlockSpec(memory_space=pltpu.VMEM)
    rows = 2 * block
    hidden = pl.pallas_call(
        spatial_kernel,
        out_shape=jax.ShapeDtypeStruct((rows, width), jnp.bfloat16),
        in_specs=[pl.BlockSpec(memory_space=pltpu.SMEM)] + [vmem] * 5,
        out_specs=vmem,
        scratch_shapes=[
            pltpu.VMEM((rows, width), jnp.bfloat16),
            pltpu.VMEM((6 * block, width), jnp.bfloat16),
            pltpu.VMEM((6 * block, width), jnp.bfloat16),
            pltpu.VMEM((rows, width), jnp.bfloat16),
            pltpu.VMEM((rows, width), jnp.bfloat16),
        ],
        compiler_params=pltpu.CompilerParams(vmem_limit_bytes=40 * 1024 * 1024),
        name="spatial",
    )(half.astype(jnp.int32).reshape(1), biases, kept_tiles, other_tiles, spatial_qkv, spatial_out)

    members = 2 * lax.axis_size("chip") * lax.axis_size("core")
    group = rows // members
    hidden = lax.all_to_all(hidden.reshape(members, group, width), COLUMN, 0, 0, tiled=True)

    half_size = HEAD // 2
    frequency = 10000.0 ** (-jnp.arange(half_size, dtype=jnp.float32) / half_size)
    order = frame_index.reshape(members // 2, 2).T.reshape(members)
    angles = order.astype(jnp.float32)[:, None] * frequency[None, :]
    cosine, sine = jnp.cos(angles), jnp.sin(angles)
    cosine = jnp.concatenate([cosine] * 4, axis=1)
    sine = jnp.concatenate([-sine, sine] * 2, axis=1)
    layer = pl.pallas_call(
        time_kernel,
        out_shape=jax.ShapeDtypeStruct((rows, width), jnp.bfloat16),
        in_specs=[vmem] * 5,
        out_specs=vmem,
        scratch_shapes=[pltpu.VMEM((rows, width), jnp.bfloat16)] * 4,
        compiler_params=pltpu.CompilerParams(vmem_limit_bytes=40 * 1024 * 1024),
        name="temporal",
    )(hidden.reshape(rows, width), cosine, sine, time_qkv, time_out)
    return lax.all_to_all(
        layer.reshape(members, group, width), ("chip", "core"), 0, 1, tiled=True
    )


def solution(mesh):
    res, frame = mesh.devices.shape
    fine = Mesh(mesh.devices.reshape(res // 2, 2, frame // 2, 2), ("pair", "half", "chip", "core"))
    placed = (P(("chip", "core"), ("pair", "half"), None), P(), P(), P(), P(), P(), P())
    return jax.shard_map(
        shards, mesh=fine, in_specs=placed, out_specs=placed[0], check_vma=False
    )
```

```python
import math

import jax
import jax.numpy as jnp
from jax import lax
from jax.experimental import pallas as pl
from jax.experimental.pallas import tpu as pltpu
from jax.sharding import Mesh
from jax.sharding import PartitionSpec as P

HEAD = 64
PAIR = 2 * HEAD
EXCLUDED = -1e30
LOG2E = 1.4426950408889634
SCALE = LOG2E / 8.0
COLUMN = ("half", "chip", "core")
VMEM = pl.BlockSpec(memory_space=pltpu.VMEM)
SMEM = pl.BlockSpec(memory_space=pltpu.SMEM)
HBM = pl.BlockSpec(memory_space=pltpu.HBM)
LIMIT = pltpu.CompilerParams(vmem_limit_bytes=24 * 1024 * 1024)


def unit_rows(rows):
    widened = rows.astype(jnp.float32)
    mean_square = jnp.mean(widened * widened, axis=-1, keepdims=True)
    return (widened * lax.rsqrt(mean_square + 1e-06)).astype(jnp.bfloat16)


def dot(left, right):
    return jnp.dot(left, right, preferred_element_type=jnp.float32)


def dot_rows(left, right):
    return lax.dot_general(
        left, right, (((1,), (1,)), ((), ())), preferred_element_type=jnp.float32
    )


def lanes_of(query, head):
    lane = lax.broadcasted_iota(jnp.int32, query.shape, 1)
    inside = (lane >= HEAD) if head else (lane < HEAD)
    return jnp.where(inside, query, jnp.zeros_like(query))


def side_by_side(first, second, rows):
    lane = lax.broadcasted_iota(jnp.int32, (rows, PAIR), 1)
    return jnp.where(lane < HEAD, first, second)


def attend(query, keys, values, biases, head, floor=None):
    scores = dot_rows(lanes_of(query, head), keys) + biases
    top = jnp.max(scores, axis=-1, keepdims=True)
    if floor is not None:
        top = jnp.maximum(top, floor)
    expo = jnp.exp2(scores - top)
    total = jnp.sum(expo, axis=-1, keepdims=True)
    return dot(expo.astype(jnp.bfloat16), values), top, total


def two_rows(bias_ref, block):
    return jnp.concatenate(
        [jnp.broadcast_to(bias_ref[y : y + 1, :], (block, bias_ref.shape[1])) for y in range(2)], axis=0
    )


def give_kernel(place_ref, act_ref, given_ref, semaphore):
    move = pltpu.make_async_copy(act_ref.at[1 - place_ref[0]], given_ref, semaphore)
    move.start()
    move.wait()


def contact_biases(place_ref, contacts_ref, early_ref, late_ref):
    half, pair = place_ref[0], place_ref[1]
    block = early_ref.shape[1] // 4
    to_other = 1 - 2 * half
    for row, (parity, moves) in enumerate(
        (
            (half, (0, -2, 2, to_other, to_other - 2, to_other + 2)),
            (1 - half, (-to_other, -to_other - 2, -to_other + 2, 0, -2, 2)),
        )
    ):
        for tile, move in enumerate(moves):
            column = jnp.clip(move + 2, 0, 4)
            flag = jnp.where(column == move + 2, contacts_ref[2 * pair + parity, column], 0)
            ref, at = (early_ref, tile) if tile < 4 else (late_ref, tile - 4)
            ref[row : row + 1, at * block : (at + 1) * block] = jnp.full(
                (1, block), jnp.where(flag > 0, 0.0, EXCLUDED), jnp.float32
            )


def rotation_tables(frame_ref, cos_ref, sin_ref):
    frames, lanes = cos_ref.shape
    row = lax.broadcasted_iota(jnp.int32, (frames, lanes), 0)
    lane = lax.broadcasted_iota(jnp.int32, (frames, lanes), 1)
    position = jnp.zeros((frames, lanes), jnp.int32)
    for j in range(frames):
        frame = 2 * (j % (frames // 2)) + j // (frames // 2)
        position = jnp.where(row == j, frame_ref[frame], position)
    half_size = HEAD // 2
    exponent = (lane % half_size).astype(jnp.float32) * (-math.log(10000.0) / half_size)
    angles = position.astype(jnp.float32) * jnp.exp(exponent)
    cos_ref[...] = jnp.cos(angles)
    sine = jnp.sin(angles)
    sin_ref[...] = jnp.where(lane % HEAD < half_size, -sine, sine)


def first_kernel(
    place_ref, contacts_ref, frame_ref, given_ref, act_ref, qkv_hbm, out_hbm, time_qkv_hbm, time_out_hbm,
    qkv_ref, out_ref, time_qkv_ref, time_out_ref, normed_ref, base_ref, query_ref, keys_ref, values_ref,
    early_ref, late_ref, cos_ref, sin_ref, sent, semaphores,
):
    half = place_ref[0]
    width = base_ref.shape[1]
    own = pltpu.make_async_copy(act_ref.at[half], base_ref, semaphores.at[0])
    own.start()
    loads = []
    for at, (source, target) in enumerate(
        ((qkv_hbm, qkv_ref), (out_hbm, out_ref), (time_qkv_hbm, time_qkv_ref), (time_out_hbm, time_out_ref))
    ):
        loads.append(pltpu.make_async_copy(source, target, semaphores.at[at + 1]))
        loads[-1].start()
    own.wait()
    normed = unit_rows(base_ref[...])
    sent[...] = normed
    store = pltpu.make_async_copy(sent, normed_ref, semaphores.at[5])
    store.start()
    loads[0].wait()
    query_ref[...] = (dot(normed, qkv_ref[:, :width]) * SCALE).astype(jnp.bfloat16)
    keys_ref[...] = dot(normed, qkv_ref[:, width : 2 * width]).astype(jnp.bfloat16)
    values_ref[...] = dot(normed, qkv_ref[:, 2 * width :]).astype(jnp.bfloat16)
    contact_biases(place_ref, contacts_ref, early_ref, late_ref)
    rotation_tables(frame_ref, cos_ref, sin_ref)
    store.wait()
    for load in loads[1:]:
        load.wait()


def early_kernel(
    bias_ref, query_in, keys_in, values_in, before_ref, after_ref, other_ref, qkv_ref,
    query_ref, sums_ref, tops_ref, totals_ref, keys, values,
):
    block, width = other_ref.shape
    query_ref[:block, :] = query_in[...]
    normed = unit_rows(other_ref[...])
    query_ref[block:, :] = (dot(normed, qkv_ref[:, :width]) * SCALE).astype(jnp.bfloat16)
    keys[:block, :] = keys_in[...]
    values[:block, :] = values_in[...]
    tiles = jnp.concatenate([before_ref[...], after_ref[...], normed], axis=0)
    keys[block:, :] = dot(tiles, qkv_ref[:, width : 2 * width]).astype(jnp.bfloat16)
    values[block:, :] = dot(tiles, qkv_ref[:, 2 * width :]).astype(jnp.bfloat16)
    biases = two_rows(bias_ref, block)
    for pair in range(width // PAIR):
        at = slice(pair * PAIR, (pair + 1) * PAIR)
        parts = [attend(query_ref[:, at], keys[:, at], values[:, at], biases, head) for head in range(2)]
        for ref, piece in ((sums_ref, 0), (tops_ref, 1), (totals_ref, 2)):
            ref[:, at] = side_by_side(parts[0][piece], parts[1][piece], 2 * block)


def late_kernel(
    place_ref, bias_ref, query_ref, sums_ref, tops_ref, totals_ref, before_ref, after_ref,
    base_ref, other_ref, qkv_ref, out_ref, hidden_ref, keys, values, mix, hidden, semaphore,
):
    half = place_ref[0]
    block, width = other_ref.shape
    tiles = unit_rows(jnp.concatenate([before_ref[...], after_ref[...]], axis=0))
    keys[...] = dot(tiles, qkv_ref[:, width : 2 * width]).astype(jnp.bfloat16)
    values[...] = dot(tiles, qkv_ref[:, 2 * width :]).astype(jnp.bfloat16)
    biases = two_rows(bias_ref, block)
    for pair in range(width // PAIR):
        at = slice(pair * PAIR, (pair + 1) * PAIR)
        floors = tops_ref[:, at]
        parts = [
            attend(
                query_ref[:, at], keys[:, at], values[:, at], biases, head,
                floors[:, head * HEAD : head * HEAD + 1],
            )
            for head in range(2)
        ]
        late = [side_by_side(parts[0][piece], parts[1][piece], 2 * block) for piece in range(3)]
        share = jnp.exp2(floors - late[1])
        total = totals_ref[:, at] * share + late[2]
        mix[:, at] = ((sums_ref[:, at] * share + late[0]) / total).astype(jnp.bfloat16)
    added = dot(mix[...], out_ref[...])
    here = pl.ds(pl.multiple_of(half * block, block), block)
    there = pl.ds(pl.multiple_of((1 - half) * block, block), block)
    hidden[here, :] = (base_ref[...].astype(jnp.float32) + added[:block]).astype(jnp.bfloat16)
    hidden[there, :] = (other_ref[...].astype(jnp.float32) + added[block:]).astype(jnp.bfloat16)
    store = pltpu.make_async_copy(hidden, hidden_ref, semaphore)
    store.start()
    store.wait()


def time_kernel(
    hidden_ref, cos_ref, sin_ref, qkv_ref, out_w_ref, layer_ref, query, keys, values, mix, layer, semaphore
):
    rows, width = hidden_ref.shape
    frames = cos_ref.shape[0]
    group = rows // frames
    normed = unit_rows(hidden_ref[...])
    cosine = jnp.concatenate(
        [jnp.broadcast_to(cos_ref[f : f + 1, :], (group, PAIR)) for f in range(frames)], axis=0
    )
    sine = jnp.concatenate(
        [jnp.broadcast_to(sin_ref[f : f + 1, :], (group, PAIR)) for f in range(frames)], axis=0
    )
    lane = lax.broadcasted_iota(jnp.int32, (rows, PAIR), 1)
    first = (lane % HEAD) < HEAD // 2

    def rotate(entries):
        entries = entries.astype(jnp.bfloat16).astype(jnp.float32)
        swapped = jnp.where(
            first, pltpu.roll(entries, PAIR - HEAD // 2, 1), pltpu.roll(entries, HEAD // 2, 1)
        )
        return entries * cosine + swapped * sine

    projected = dot(normed, qkv_ref[:, : 2 * width])
    for pair in range(width // PAIR):
        at = slice(pair * PAIR, (pair + 1) * PAIR)
        query[:, at] = (rotate(projected[:, at]) * SCALE).astype(jnp.bfloat16)
        keys[:, at] = rotate(projected[:, width + pair * PAIR : width + (pair + 1) * PAIR]).astype(jnp.bfloat16)
    values[...] = dot(normed, qkv_ref[:, 2 * width :]).astype(jnp.bfloat16)
    row = lax.broadcasted_iota(jnp.int32, (rows, rows), 0)
    column = lax.broadcasted_iota(jnp.int32, (rows, rows), 1)
    biases = jnp.where(row % group == column % group, 0.0, EXCLUDED)
    for pair in range(width // PAIR):
        at = slice(pair * PAIR, (pair + 1) * PAIR)
        parts = [attend(query[:, at], keys[:, at], values[:, at], biases, head) for head in range(2)]
        mix[:, at] = side_by_side(
            parts[0][0] / parts[0][2], parts[1][0] / parts[1][2], rows
        ).astype(jnp.bfloat16)
    added = (hidden_ref[...].astype(jnp.float32) + dot(mix[...], out_w_ref[...])).astype(jnp.bfloat16)
    per_half = frames // 2
    for j in range(frames):
        frame = 2 * (j % per_half) + j // per_half
        layer[frame * group : (frame + 1) * group, :] = added[j * group : (j + 1) * group, :]
    store = pltpu.make_async_copy(layer, layer_ref, semaphore)
    store.start()
    store.wait()


def shards(activations, contacts, frame_index, spatial_qkv, spatial_out, time_qkv, time_out):
    frames_dev, block, width = activations.shape
    pairs = lax.axis_size("pair")
    pair = lax.axis_index("pair")
    half = lax.axis_index("half")
    place = jnp.stack([half, pair]).astype(jnp.int32)
    activations, spatial_qkv, spatial_out, time_qkv, time_out = (
        pltpu.with_memory_space_constraint(x, pltpu.HBM)
        for x in (activations, spatial_qkv, spatial_out, time_qkv, time_out)
    )
    rows = 2 * block
    bf16, f32 = jnp.bfloat16, jnp.float32
    given = pl.pallas_call(
        give_kernel,
        out_shape=pltpu.HBM((block, width), bf16),
        in_specs=[SMEM, HBM],
        out_specs=HBM,
        scratch_shapes=[pltpu.SemaphoreType.DMA],
        name="give",
    )(place, activations)
    other = lax.ppermute(given, "half", [(0, 1), (1, 0)])

    def from_neighbours(tile):
        before = lax.ppermute(tile, "pair", [(i, (i + 1) % pairs) for i in range(pairs)])
        after = lax.ppermute(tile, "pair", [((i + 1) % pairs, i) for i in range(pairs)])
        return before, after

    tile_in_vmem = pltpu.VMEM((block, width), bf16)
    weights = (spatial_qkv, spatial_out, time_qkv, time_out)
    members = 2 * lax.axis_size("chip") * lax.axis_size("core")
    table = pltpu.VMEM((members, PAIR), f32)
    *weights, normed, base, query, keys, values, early_bias, late_bias, cosine, sine = pl.pallas_call(
        first_kernel,
        out_shape=tuple(pltpu.VMEM(w.shape, bf16) for w in weights)
        + (pltpu.HBM((block, width), bf16),)
        + (tile_in_vmem,) * 4
        + (pltpu.VMEM((2, 4 * block), f32), pltpu.VMEM((2, 2 * block), f32), table, table),
        in_specs=[SMEM] * 3 + [HBM] * 6,
        out_specs=(VMEM,) * 4 + (HBM,) + (VMEM,) * 8,
        scratch_shapes=[tile_in_vmem, pltpu.SemaphoreType.DMA((6,))],
        compiler_params=LIMIT,
        cost_estimate=pl.CostEstimate(flops=2 * block * width * 3 * width, bytes_accessed=10_000_000, transcendentals=0),
        name="first",
    )(place, contacts, frame_index, pltpu.with_memory_space_constraint(given, pltpu.HBM), activations, *weights)
    spatial_qkv, spatial_out, time_qkv, time_out = weights
    kept_before, kept_after = from_neighbours(normed)
    other_before, other_after = from_neighbours(other)

    wide = pltpu.VMEM((rows, width), f32)
    query, sums, tops, totals = pl.pallas_call(
        early_kernel,
        out_shape=(pltpu.VMEM((rows, width), bf16), wide, wide, wide),
        in_specs=[VMEM] * 8,
        out_specs=(VMEM,) * 4,
        scratch_shapes=[pltpu.VMEM((4 * block, width), bf16)] * 2,
        compiler_params=LIMIT,
        cost_estimate=pl.CostEstimate(flops=4_000_000_000, bytes_accessed=4_000_000, transcendentals=2_000_000),
        name="early",
    )(early_bias, query, keys, values, kept_before, kept_after, other, spatial_qkv)
    hidden = pl.pallas_call(
        late_kernel,
        out_shape=pltpu.HBM((rows, width), bf16),
        in_specs=[SMEM] + [VMEM] * 11,
        out_specs=HBM,
        scratch_shapes=[pltpu.VMEM((rows, width), bf16)] * 4 + [pltpu.SemaphoreType.DMA],
        compiler_params=LIMIT,
        name="late",
    )(
        place, late_bias, query, sums, tops, totals, other_before, other_after,
        base, other, spatial_qkv, spatial_out,
    )

    group = rows // members
    hidden = lax.all_to_all(hidden.reshape(members, group, width), COLUMN, 0, 0, tiled=True)

    layer = pl.pallas_call(
        time_kernel,
        out_shape=pltpu.HBM((rows, width), bf16),
        in_specs=[VMEM] * 5,
        out_specs=HBM,
        scratch_shapes=[pltpu.VMEM((rows, width), bf16)] * 5 + [pltpu.SemaphoreType.DMA],
        compiler_params=LIMIT,
        name="temporal",
    )(hidden.reshape(rows, width), cosine, sine, time_qkv, time_out)
    return lax.all_to_all(
        layer.reshape(members, group, width), ("chip", "core"), 0, 1, tiled=True
    )


def solution(mesh):
    res, frame = mesh.devices.shape
    fine = Mesh(mesh.devices.reshape(res // 2, 2, frame // 2, 2), ("pair", "half", "chip", "core"))
    placed = (P(("chip", "core"), ("pair", "half"), None), P(), P(), P(), P(), P(), P())
    return jax.shard_map(
        shards, mesh=fine, in_specs=placed, out_specs=placed[0], check_vma=False
    )
```

```python
import math

import jax
import jax.numpy as jnp
from jax import lax
from jax.experimental import pallas as pl
from jax.experimental.pallas import tpu as pltpu
from jax.sharding import Mesh
from jax.sharding import PartitionSpec as P

HEAD = 64
PAIR = 2 * HEAD
EXCLUDED = -1e30
LOG2E = 1.4426950408889634
SCALE = LOG2E / 8.0
COLUMN = ("half", "chip", "core")
VMEM = pl.BlockSpec(memory_space=pltpu.VMEM)
SMEM = pl.BlockSpec(memory_space=pltpu.SMEM)
HBM = pl.BlockSpec(memory_space=pltpu.HBM)
LIMIT = pltpu.CompilerParams(vmem_limit_bytes=24 * 1024 * 1024)


def unit_rows(rows):
    widened = rows.astype(jnp.float32)
    mean_square = jnp.mean(widened * widened, axis=-1, keepdims=True)
    return (widened * lax.rsqrt(mean_square + 1e-06)).astype(jnp.bfloat16)


def dot(left, right):
    return jnp.dot(left, right, preferred_element_type=jnp.float32)


def dot_rows(left, right):
    return lax.dot_general(
        left, right, (((1,), (1,)), ((), ())), preferred_element_type=jnp.float32
    )


def lanes_of(query, head):
    lane = lax.broadcasted_iota(jnp.int32, query.shape, 1)
    inside = (lane >= HEAD) if head else (lane < HEAD)
    return jnp.where(inside, query, jnp.zeros_like(query))


def side_by_side(first, second, rows):
    lane = lax.broadcasted_iota(jnp.int32, (rows, PAIR), 1)
    return jnp.where(lane < HEAD, first, second)


def attend(query, keys, values, biases, head, floor=None):
    scores = dot_rows(lanes_of(query, head), keys) + biases
    top = jnp.max(scores, axis=-1, keepdims=True)
    if floor is not None:
        top = jnp.maximum(top, floor)
    expo = jnp.exp2(scores - top)
    total = jnp.sum(expo, axis=-1, keepdims=True)
    return dot(expo.astype(jnp.bfloat16), values), top, total


def two_rows(bias_ref, block):
    return jnp.concatenate(
        [jnp.broadcast_to(bias_ref[y : y + 1, :], (block, bias_ref.shape[1])) for y in range(2)], axis=0
    )


def give_kernel(act_ref, given_ref, semaphore):
    move = pltpu.make_async_copy(act_ref.at[1 - lax.axis_index("half")], given_ref, semaphore)
    move.start()
    move.wait()


def contact_biases(contacts_ref, early_ref, late_ref):
    half, pair = lax.axis_index("half"), lax.axis_index("pair")
    block = early_ref.shape[1] // 4
    to_other = 1 - 2 * half
    for row, (parity, moves) in enumerate(
        (
            (half, (0, -2, 2, to_other, to_other - 2, to_other + 2)),
            (1 - half, (-to_other, -to_other - 2, -to_other + 2, 0, -2, 2)),
        )
    ):
        for tile, move in enumerate(moves):
            column = jnp.clip(move + 2, 0, 4)
            flag = jnp.where(column == move + 2, contacts_ref[2 * pair + parity, column], 0)
            ref, at = (early_ref, tile) if tile < 4 else (late_ref, tile - 4)
            ref[row : row + 1, at * block : (at + 1) * block] = jnp.full(
                (1, block), jnp.where(flag > 0, 0.0, EXCLUDED), jnp.float32
            )


def rotation_tables(frame_ref, cos_ref, sin_ref):
    frames, lanes = cos_ref.shape
    row = lax.broadcasted_iota(jnp.int32, (frames, lanes), 0)
    lane = lax.broadcasted_iota(jnp.int32, (frames, lanes), 1)
    position = jnp.zeros((frames, lanes), jnp.int32)
    for j in range(frames):
        frame = 2 * (j % (frames // 2)) + j // (frames // 2)
        position = jnp.where(row == j, frame_ref[frame], position)
    half_size = HEAD // 2
    exponent = (lane % half_size).astype(jnp.float32) * (-math.log(10000.0) / half_size)
    angles = position.astype(jnp.float32) * jnp.exp(exponent)
    cos_ref[...] = jnp.cos(angles)
    sine = jnp.sin(angles)
    sin_ref[...] = jnp.where(lane % HEAD < half_size, -sine, sine)


def first_kernel(
    contacts_ref, frame_ref, given_ref, act_ref, qkv_hbm, out_hbm, time_qkv_hbm, time_out_hbm,
    qkv_ref, out_ref, time_qkv_ref, time_out_ref, normed_ref, base_ref, query_ref, keys_ref, values_ref,
    early_ref, late_ref, cos_ref, sin_ref, semaphores,
):
    half = lax.axis_index("half")
    width = base_ref.shape[1]
    own = pltpu.make_async_copy(act_ref.at[half], base_ref, semaphores.at[0])
    own.start()
    loads = []
    for at, (source, target) in enumerate(
        ((qkv_hbm, qkv_ref), (out_hbm, out_ref), (time_qkv_hbm, time_qkv_ref), (time_out_hbm, time_out_ref))
    ):
        loads.append(pltpu.make_async_copy(source, target, semaphores.at[at + 1]))
        loads[-1].start()
    own.wait()
    normed = unit_rows(base_ref[...])
    normed_ref[...] = normed
    loads[0].wait()
    query_ref[...] = (dot(normed, qkv_ref[:, :width]) * SCALE).astype(jnp.bfloat16)
    keys_ref[...] = dot(normed, qkv_ref[:, width : 2 * width]).astype(jnp.bfloat16)
    values_ref[...] = dot(normed, qkv_ref[:, 2 * width :]).astype(jnp.bfloat16)
    contact_biases(contacts_ref, early_ref, late_ref)
    rotation_tables(frame_ref, cos_ref, sin_ref)
    for load in loads[1:]:
        load.wait()


def early_kernel(
    bias_ref, query_in, keys_in, values_in, before_ref, after_ref, other_ref, qkv_ref,
    query_ref, sums_ref, tops_ref, totals_ref, keys, values,
):
    block, width = other_ref.shape
    query_ref[:block, :] = query_in[...]
    normed = unit_rows(other_ref[...])
    query_ref[block:, :] = (dot(normed, qkv_ref[:, :width]) * SCALE).astype(jnp.bfloat16)
    keys[:block, :] = keys_in[...]
    values[:block, :] = values_in[...]
    tiles = jnp.concatenate([before_ref[...], after_ref[...], normed], axis=0)
    keys[block:, :] = dot(tiles, qkv_ref[:, width : 2 * width]).astype(jnp.bfloat16)
    values[block:, :] = dot(tiles, qkv_ref[:, 2 * width :]).astype(jnp.bfloat16)
    biases = two_rows(bias_ref, block)
    for pair in range(width // PAIR):
        at = slice(pair * PAIR, (pair + 1) * PAIR)
        parts = [attend(query_ref[:, at], keys[:, at], values[:, at], biases, head) for head in range(2)]
        for ref, piece in ((sums_ref, 0), (tops_ref, 1), (totals_ref, 2)):
            ref[:, at] = side_by_side(parts[0][piece], parts[1][piece], 2 * block)


def late_kernel(
    bias_ref, query_ref, sums_ref, tops_ref, totals_ref, before_ref, after_ref,
    base_ref, other_ref, qkv_ref, out_ref, hidden_ref, keys, values, mix, hidden, semaphore,
):
    half = lax.axis_index("half")
    block, width = other_ref.shape
    tiles = unit_rows(jnp.concatenate([before_ref[...], after_ref[...]], axis=0))
    keys[...] = dot(tiles, qkv_ref[:, width : 2 * width]).astype(jnp.bfloat16)
    values[...] = dot(tiles, qkv_ref[:, 2 * width :]).astype(jnp.bfloat16)
    biases = two_rows(bias_ref, block)
    for pair in range(width // PAIR):
        at = slice(pair * PAIR, (pair + 1) * PAIR)
        floors = tops_ref[:, at]
        parts = [
            attend(
                query_ref[:, at], keys[:, at], values[:, at], biases, head,
                floors[:, head * HEAD : head * HEAD + 1],
            )
            for head in range(2)
        ]
        late = [side_by_side(parts[0][piece], parts[1][piece], 2 * block) for piece in range(3)]
        share = jnp.exp2(floors - late[1])
        total = totals_ref[:, at] * share + late[2]
        mix[:, at] = ((sums_ref[:, at] * share + late[0]) / total).astype(jnp.bfloat16)
    added = dot(mix[...], out_ref[...])
    here = pl.ds(pl.multiple_of(half * block, block), block)
    there = pl.ds(pl.multiple_of((1 - half) * block, block), block)
    hidden[here, :] = (base_ref[...].astype(jnp.float32) + added[:block]).astype(jnp.bfloat16)
    hidden[there, :] = (other_ref[...].astype(jnp.float32) + added[block:]).astype(jnp.bfloat16)
    store = pltpu.make_async_copy(hidden, hidden_ref, semaphore)
    store.start()
    store.wait()


def time_kernel(
    hidden_ref, cos_ref, sin_ref, qkv_ref, out_w_ref, layer_ref, query, keys, values, mix, layer, semaphore
):
    rows, width = hidden_ref.shape
    frames = cos_ref.shape[0]
    group = rows // frames
    normed = unit_rows(hidden_ref[...])
    cosine = jnp.concatenate(
        [jnp.broadcast_to(cos_ref[f : f + 1, :], (group, PAIR)) for f in range(frames)], axis=0
    )
    sine = jnp.concatenate(
        [jnp.broadcast_to(sin_ref[f : f + 1, :], (group, PAIR)) for f in range(frames)], axis=0
    )
    lane = lax.broadcasted_iota(jnp.int32, (rows, PAIR), 1)
    first = (lane % HEAD) < HEAD // 2

    def rotate(entries):
        entries = entries.astype(jnp.bfloat16).astype(jnp.float32)
        swapped = jnp.where(
            first, pltpu.roll(entries, PAIR - HEAD // 2, 1), pltpu.roll(entries, HEAD // 2, 1)
        )
        return entries * cosine + swapped * sine

    projected = dot(normed, qkv_ref[:, : 2 * width])
    for pair in range(width // PAIR):
        at = slice(pair * PAIR, (pair + 1) * PAIR)
        query[:, at] = (rotate(projected[:, at]) * SCALE).astype(jnp.bfloat16)
        keys[:, at] = rotate(projected[:, width + pair * PAIR : width + (pair + 1) * PAIR]).astype(jnp.bfloat16)
    values[...] = dot(normed, qkv_ref[:, 2 * width :]).astype(jnp.bfloat16)
    row = lax.broadcasted_iota(jnp.int32, (rows, rows), 0)
    column = lax.broadcasted_iota(jnp.int32, (rows, rows), 1)
    biases = jnp.where(row % group == column % group, 0.0, EXCLUDED)
    for pair in range(width // PAIR):
        at = slice(pair * PAIR, (pair + 1) * PAIR)
        parts = [attend(query[:, at], keys[:, at], values[:, at], biases, head) for head in range(2)]
        mix[:, at] = side_by_side(
            parts[0][0] / parts[0][2], parts[1][0] / parts[1][2], rows
        ).astype(jnp.bfloat16)
    added = (hidden_ref[...].astype(jnp.float32) + dot(mix[...], out_w_ref[...])).astype(jnp.bfloat16)
    per_half = frames // 2
    for j in range(frames):
        frame = 2 * (j % per_half) + j // per_half
        layer[frame * group : (frame + 1) * group, :] = added[j * group : (j + 1) * group, :]
    store = pltpu.make_async_copy(layer, layer_ref, semaphore)
    store.start()
    store.wait()


def shards(activations, contacts, frame_index, spatial_qkv, spatial_out, time_qkv, time_out):
    frames_dev, block, width = activations.shape
    pairs = lax.axis_size("pair")
    activations, spatial_qkv, spatial_out, time_qkv, time_out = (
        pltpu.with_memory_space_constraint(x, pltpu.HBM)
        for x in (activations, spatial_qkv, spatial_out, time_qkv, time_out)
    )
    rows = 2 * block
    bf16, f32 = jnp.bfloat16, jnp.float32
    given = pl.pallas_call(
        give_kernel,
        out_shape=pltpu.VMEM((block, width), bf16),
        in_specs=[HBM],
        out_specs=VMEM,
        scratch_shapes=[pltpu.SemaphoreType.DMA],
        name="give",
    )(activations)
    other = lax.ppermute(given, "half", [(0, 1), (1, 0)])

    def from_neighbours(tile):
        before = lax.ppermute(tile, "pair", [(i, (i + 1) % pairs) for i in range(pairs)])
        after = lax.ppermute(tile, "pair", [((i + 1) % pairs, i) for i in range(pairs)])
        return before, after

    tile_in_vmem = pltpu.VMEM((block, width), bf16)
    weights = (spatial_qkv, spatial_out, time_qkv, time_out)
    members = 2 * lax.axis_size("chip") * lax.axis_size("core")
    table = pltpu.VMEM((members, PAIR), f32)
    *weights, normed, base, query, keys, values, early_bias, late_bias, cosine, sine = pl.pallas_call(
        first_kernel,
        out_shape=tuple(pltpu.VMEM(w.shape, bf16) for w in weights)
        + (tile_in_vmem,)
        + (tile_in_vmem,) * 4
        + (pltpu.VMEM((2, 4 * block), f32), pltpu.VMEM((2, 2 * block), f32), table, table),
        in_specs=[SMEM] * 2 + [VMEM] + [HBM] * 5,
        out_specs=(VMEM,) * 13,
        scratch_shapes=[pltpu.SemaphoreType.DMA((5,))],
        compiler_params=LIMIT,
        cost_estimate=pl.CostEstimate(flops=2 * block * width * 3 * width, bytes_accessed=10_000_000, transcendentals=0),
        name="first",
    )(contacts, frame_index, given, activations, *weights)
    spatial_qkv, spatial_out, time_qkv, time_out = weights
    kept_before, kept_after = from_neighbours(normed)
    other_before, other_after = from_neighbours(other)

    wide = pltpu.VMEM((rows, width), f32)
    query, sums, tops, totals = pl.pallas_call(
        early_kernel,
        out_shape=(pltpu.VMEM((rows, width), bf16), wide, wide, wide),
        in_specs=[VMEM] * 8,
        out_specs=(VMEM,) * 4,
        scratch_shapes=[pltpu.VMEM((4 * block, width), bf16)] * 2,
        compiler_params=LIMIT,
        cost_estimate=pl.CostEstimate(flops=4_000_000_000, bytes_accessed=4_000_000, transcendentals=2_000_000),
        name="early",
    )(early_bias, query, keys, values, kept_before, kept_after, other, spatial_qkv)
    hidden = pl.pallas_call(
        late_kernel,
        out_shape=pltpu.HBM((rows, width), bf16),
        in_specs=[VMEM] * 11,
        out_specs=HBM,
        scratch_shapes=[pltpu.VMEM((rows, width), bf16)] * 4 + [pltpu.SemaphoreType.DMA],
        compiler_params=LIMIT,
        name="late",
    )(
        late_bias, query, sums, tops, totals, other_before, other_after,
        base, other, spatial_qkv, spatial_out,
    )

    group = rows // members
    hidden = lax.all_to_all(hidden.reshape(members, group, width), COLUMN, 0, 0, tiled=True)

    layer = pl.pallas_call(
        time_kernel,
        out_shape=pltpu.HBM((rows, width), bf16),
        in_specs=[VMEM] * 5,
        out_specs=HBM,
        scratch_shapes=[pltpu.VMEM((rows, width), bf16)] * 5 + [pltpu.SemaphoreType.DMA],
        compiler_params=LIMIT,
        name="temporal",
    )(hidden.reshape(rows, width), cosine, sine, time_qkv, time_out)
    return lax.all_to_all(
        layer.reshape(members, group, width), ("chip", "core"), 0, 1, tiled=True
    )


def solution(mesh):
    res, frame = mesh.devices.shape
    fine = Mesh(mesh.devices.reshape(res // 2, 2, frame // 2, 2), ("pair", "half", "chip", "core"))
    placed = (P(("chip", "core"), ("pair", "half"), None), P(), P(), P(), P(), P(), P())
    return jax.shard_map(
        shards, mesh=fine, in_specs=placed, out_specs=placed[0], check_vma=False
    )
```

```python
import math

import jax
import jax.numpy as jnp
from jax import lax
from jax.experimental import pallas as pl
from jax.experimental.pallas import tpu as pltpu
from jax.sharding import Mesh
from jax.sharding import PartitionSpec as P

HEAD = 64
PAIR = 2 * HEAD
EXCLUDED = -1e30
LOG2E = 1.4426950408889634
SCALE = LOG2E / 8.0
COLUMN = ("half", "chip", "core")
VMEM = pl.BlockSpec(memory_space=pltpu.VMEM)
SMEM = pl.BlockSpec(memory_space=pltpu.SMEM)
HBM = pl.BlockSpec(memory_space=pltpu.HBM)
LIMIT = pltpu.CompilerParams(vmem_limit_bytes=24 * 1024 * 1024)


def unit_rows(rows):
    widened = rows.astype(jnp.float32)
    mean_square = jnp.mean(widened * widened, axis=-1, keepdims=True)
    return (widened * lax.rsqrt(mean_square + 1e-06)).astype(jnp.bfloat16)


def dot(left, right):
    return jnp.dot(left, right, preferred_element_type=jnp.float32)


def dot_rows(left, right):
    return lax.dot_general(
        left, right, (((1,), (1,)), ((), ())), preferred_element_type=jnp.float32
    )


def by_head(pair_query):
    lane = lax.broadcasted_iota(jnp.int32, pair_query.shape, 1)
    nothing = jnp.zeros_like(pair_query)
    return jnp.concatenate(
        [jnp.where(lane < HEAD, pair_query, nothing), jnp.where(lane < HEAD, nothing, pair_query)], axis=0
    )


def side_by_side(stacked):
    rows = stacked.shape[0] // 2
    lane = lax.broadcasted_iota(jnp.int32, (rows, PAIR), 1)
    return jnp.where(lane < HEAD, stacked[:rows, :PAIR], stacked[rows:, :PAIR])


def two_rows(bias_ref, block):
    halves = [jnp.broadcast_to(bias_ref[y : y + 1, :], (block, bias_ref.shape[1])) for y in range(2)]
    return jnp.concatenate(halves * 2, axis=0)


def attend(stacked_query, keys, values, pairs, biases, finish, floors=None):
    width = keys.shape[0]

    def scores_of(pair):
        return dot_rows(stacked_query[pair], keys[:, pair * PAIR : (pair + 1) * PAIR]) + biases

    scores = scores_of(0)
    for pair in range(pairs):
        ahead = scores_of(pair + 1) if pair + 1 < pairs else None
        top = jnp.broadcast_to(jnp.max(scores, axis=-1, keepdims=True), (scores.shape[0], PAIR))
        if floors is not None:
            top = jnp.maximum(top, floors[pair])
        expo = jnp.exp2(scores - jnp.concatenate([top] * (width // PAIR), axis=1)).astype(jnp.bfloat16)
        finish(pair, top, dot(expo, values[pair]))
        scores = ahead


def give_kernel(act_ref, given_ref, semaphore):
    move = pltpu.make_async_copy(act_ref.at[1 - lax.axis_index("half")], given_ref, semaphore)
    move.start()
    move.wait()


def contact_biases(contacts_ref, early_ref, late_ref):
    half, pair = lax.axis_index("half"), lax.axis_index("pair")
    block = early_ref.shape[1] // 4
    to_other = 1 - 2 * half
    for row, (parity, moves) in enumerate(
        (
            (half, (0, -2, 2, to_other, to_other - 2, to_other + 2)),
            (1 - half, (-to_other, -to_other - 2, -to_other + 2, 0, -2, 2)),
        )
    ):
        for tile, move in enumerate(moves):
            column = jnp.clip(move + 2, 0, 4)
            flag = jnp.where(column == move + 2, contacts_ref[2 * pair + parity, column], 0)
            ref, at = (early_ref, tile) if tile < 4 else (late_ref, tile - 4)
            ref[row : row + 1, at * block : (at + 1) * block] = jnp.full(
                (1, block), jnp.where(flag > 0, 0.0, EXCLUDED), jnp.float32
            )


def rotation_tables(frame_ref, cos_ref, sin_ref):
    frames, lanes = cos_ref.shape
    row = lax.broadcasted_iota(jnp.int32, (frames, lanes), 0)
    lane = lax.broadcasted_iota(jnp.int32, (frames, lanes), 1)
    position = jnp.zeros((frames, lanes), jnp.int32)
    for j in range(frames):
        frame = 2 * (j % (frames // 2)) + j // (frames // 2)
        position = jnp.where(row == j, frame_ref[frame], position)
    half_size = HEAD // 2
    exponent = (lane % half_size).astype(jnp.float32) * (-math.log(10000.0) / half_size)
    angles = position.astype(jnp.float32) * jnp.exp(exponent)
    cos_ref[...] = jnp.cos(angles)
    sine = jnp.sin(angles)
    sin_ref[...] = jnp.where(lane % HEAD < half_size, -sine, sine)


def first_kernel(
    contacts_ref, frame_ref, given_ref, act_ref, qkv_hbm, out_hbm, time_qkv_hbm, time_out_hbm,
    qkv_ref, out_ref, time_qkv_ref, time_out_ref, normed_ref, base_ref, query_ref, keys_ref, values_ref,
    early_ref, late_ref, cos_ref, sin_ref, semaphores,
):
    half = lax.axis_index("half")
    width = base_ref.shape[1]
    own = pltpu.make_async_copy(act_ref.at[half], base_ref, semaphores.at[0])
    own.start()
    loads = []
    for at, (source, target) in enumerate(
        ((qkv_hbm, qkv_ref), (out_hbm, out_ref), (time_qkv_hbm, time_qkv_ref), (time_out_hbm, time_out_ref))
    ):
        loads.append(pltpu.make_async_copy(source, target, semaphores.at[at + 1]))
        loads[-1].start()
    own.wait()
    normed = unit_rows(base_ref[...])
    normed_ref[...] = normed
    loads[0].wait()
    query_ref[...] = (dot(normed, qkv_ref[:, :width]) * SCALE).astype(jnp.bfloat16)
    keys_ref[...] = dot(normed, qkv_ref[:, width : 2 * width]).astype(jnp.bfloat16)
    values_ref[...] = dot(normed, qkv_ref[:, 2 * width :]).astype(jnp.bfloat16)
    contact_biases(contacts_ref, early_ref, late_ref)
    rotation_tables(frame_ref, cos_ref, sin_ref)
    for load in loads[1:]:
        load.wait()


def early_kernel(
    bias_ref, query_in, keys_in, values_in, before_ref, after_ref, other_ref, qkv_ref,
    query_ref, sums_ref, tops_ref, totals_ref, keys, values,
):
    block, width = other_ref.shape
    pairs = width // PAIR
    normed = unit_rows(other_ref[...])
    query = (dot(normed, qkv_ref[:, :width]) * SCALE).astype(jnp.bfloat16)
    keys[:block, :] = keys_in[...]
    tiles = jnp.concatenate([before_ref[...], after_ref[...], normed], axis=0)
    keys[block:, :] = dot(tiles, qkv_ref[:, width : 2 * width]).astype(jnp.bfloat16)
    fresh = dot(tiles, qkv_ref[:, 2 * width :]).astype(jnp.bfloat16)
    for pair in range(pairs):
        at = slice(pair * PAIR, (pair + 1) * PAIR)
        values[pair, :block, :PAIR] = values_in[:, at]
        values[pair, block:, :PAIR] = fresh[:, at]
        values[pair, :, PAIR:] = jnp.ones((4 * block, PAIR), jnp.bfloat16)
        query_ref[pair] = by_head(jnp.concatenate([query_in[:, at], query[:, at]], axis=0))

    def finish(pair, top, product):
        at = slice(pair * PAIR, (pair + 1) * PAIR)
        tops_ref[pair] = top
        sums_ref[:, at] = side_by_side(product)
        totals_ref[:, at] = side_by_side(product[:, PAIR:])

    attend(query_ref, keys, values, pairs, two_rows(bias_ref, block), finish)


def late_kernel(
    bias_ref, query_ref, sums_ref, tops_ref, totals_ref, before_ref, after_ref,
    base_ref, other_ref, qkv_ref, out_ref, hidden_ref, keys, values, mix, hidden, semaphore,
):
    half = lax.axis_index("half")
    block, width = other_ref.shape
    pairs = width // PAIR
    tiles = unit_rows(jnp.concatenate([before_ref[...], after_ref[...]], axis=0))
    keys[...] = dot(tiles, qkv_ref[:, width : 2 * width]).astype(jnp.bfloat16)
    fresh = dot(tiles, qkv_ref[:, 2 * width :]).astype(jnp.bfloat16)
    for pair in range(pairs):
        values[pair, :, :PAIR] = fresh[:, pair * PAIR : (pair + 1) * PAIR]
        values[pair, :, PAIR:] = jnp.ones((2 * block, PAIR), jnp.bfloat16)

    def finish(pair, top, product):
        at = slice(pair * PAIR, (pair + 1) * PAIR)
        share = side_by_side(jnp.exp2(tops_ref[pair] - top))
        total = totals_ref[:, at] * share + side_by_side(product[:, PAIR:])
        mix[:, at] = ((sums_ref[:, at] * share + side_by_side(product)) / total).astype(jnp.bfloat16)

    attend(query_ref, keys, values, pairs, two_rows(bias_ref, block), finish, tops_ref)
    added = dot(mix[...], out_ref[...])
    here = pl.ds(pl.multiple_of(half * block, block), block)
    there = pl.ds(pl.multiple_of((1 - half) * block, block), block)
    hidden[here, :] = (base_ref[...].astype(jnp.float32) + added[:block]).astype(jnp.bfloat16)
    hidden[there, :] = (other_ref[...].astype(jnp.float32) + added[block:]).astype(jnp.bfloat16)
    store = pltpu.make_async_copy(hidden, hidden_ref, semaphore)
    store.start()
    store.wait()


def time_kernel(
    hidden_ref, cos_ref, sin_ref, qkv_ref, out_w_ref, layer_ref, query, keys, values, mix, layer, semaphore
):
    rows, width = hidden_ref.shape
    frames = cos_ref.shape[0]
    group = rows // frames
    normed = unit_rows(hidden_ref[...])
    cosine = jnp.concatenate(
        [jnp.broadcast_to(cos_ref[f : f + 1, :], (group, PAIR)) for f in range(frames)], axis=0
    )
    sine = jnp.concatenate(
        [jnp.broadcast_to(sin_ref[f : f + 1, :], (group, PAIR)) for f in range(frames)], axis=0
    )
    lane = lax.broadcasted_iota(jnp.int32, (rows, PAIR), 1)
    first = (lane % HEAD) < HEAD // 2

    def rotate(entries):
        entries = entries.astype(jnp.bfloat16).astype(jnp.float32)
        swapped = jnp.where(
            first, pltpu.roll(entries, PAIR - HEAD // 2, 1), pltpu.roll(entries, HEAD // 2, 1)
        )
        return entries * cosine + swapped * sine

    pairs = width // PAIR
    projected = dot(normed, qkv_ref[...])
    for pair in range(pairs):
        at = slice(pair * PAIR, (pair + 1) * PAIR)
        query[pair] = by_head((rotate(projected[:, at]) * SCALE).astype(jnp.bfloat16))
        keys[:, at] = rotate(projected[:, width + pair * PAIR : width + (pair + 1) * PAIR]).astype(jnp.bfloat16)
        values[pair, :, :PAIR] = projected[:, 2 * width + pair * PAIR : 2 * width + (pair + 1) * PAIR].astype(jnp.bfloat16)
        values[pair, :, PAIR:] = jnp.ones((rows, PAIR), jnp.bfloat16)
    row = lax.broadcasted_iota(jnp.int32, (2 * rows, rows), 0)
    column = lax.broadcasted_iota(jnp.int32, (2 * rows, rows), 1)
    biases = jnp.where(row % group == column % group, 0.0, EXCLUDED)

    def finish(pair, top, product):
        mixed = side_by_side(product) / side_by_side(product[:, PAIR:])
        mix[:, pair * PAIR : (pair + 1) * PAIR] = mixed.astype(jnp.bfloat16)

    attend(query, keys, values, pairs, biases, finish)
    added = (hidden_ref[...].astype(jnp.float32) + dot(mix[...], out_w_ref[...])).astype(jnp.bfloat16)
    per_half = frames // 2
    for j in range(frames):
        frame = 2 * (j % per_half) + j // per_half
        layer[frame * group : (frame + 1) * group, :] = added[j * group : (j + 1) * group, :]
    store = pltpu.make_async_copy(layer, layer_ref, semaphore)
    store.start()
    store.wait()


def shards(activations, contacts, frame_index, spatial_qkv, spatial_out, time_qkv, time_out):
    frames_dev, block, width = activations.shape
    pairs = lax.axis_size("pair")
    activations, spatial_qkv, spatial_out, time_qkv, time_out = (
        pltpu.with_memory_space_constraint(x, pltpu.HBM)
        for x in (activations, spatial_qkv, spatial_out, time_qkv, time_out)
    )
    rows = 2 * block
    bf16, f32 = jnp.bfloat16, jnp.float32
    given = pl.pallas_call(
        give_kernel,
        out_shape=pltpu.VMEM((block, width), bf16),
        in_specs=[HBM],
        out_specs=VMEM,
        scratch_shapes=[pltpu.SemaphoreType.DMA],
        name="give",
    )(activations)
    other = lax.ppermute(given, "half", [(0, 1), (1, 0)])

    def from_neighbours(tile):
        before = lax.ppermute(tile, "pair", [(i, (i + 1) % pairs) for i in range(pairs)])
        after = lax.ppermute(tile, "pair", [((i + 1) % pairs, i) for i in range(pairs)])
        return before, after

    tile_in_vmem = pltpu.VMEM((block, width), bf16)
    weights = (spatial_qkv, spatial_out, time_qkv, time_out)
    members = 2 * lax.axis_size("chip") * lax.axis_size("core")
    table = pltpu.VMEM((members, PAIR), f32)
    *weights, normed, base, query, keys, values, early_bias, late_bias, cosine, sine = pl.pallas_call(
        first_kernel,
        out_shape=tuple(pltpu.VMEM(w.shape, bf16) for w in weights)
        + (tile_in_vmem,)
        + (tile_in_vmem,) * 4
        + (pltpu.VMEM((2, 4 * block), f32), pltpu.VMEM((2, 2 * block), f32), table, table),
        in_specs=[SMEM] * 2 + [VMEM] + [HBM] * 5,
        out_specs=(VMEM,) * 13,
        scratch_shapes=[pltpu.SemaphoreType.DMA((5,))],
        compiler_params=LIMIT,
        cost_estimate=pl.CostEstimate(flops=2 * block * width * 3 * width, bytes_accessed=10_000_000, transcendentals=0),
        name="first",
    )(contacts, frame_index, given, activations, *weights)
    spatial_qkv, spatial_out, time_qkv, time_out = weights
    kept_before, kept_after = from_neighbours(normed)
    other_before, other_after = from_neighbours(other)

    wide = pltpu.VMEM((rows, width), f32)
    tops_shape = pltpu.VMEM((width // PAIR, 2 * rows, PAIR), f32)
    query, sums, tops, totals = pl.pallas_call(
        early_kernel,
        out_shape=(pltpu.VMEM((width // PAIR, 2 * rows, PAIR), bf16), wide, tops_shape, wide),
        in_specs=[VMEM] * 8,
        out_specs=(VMEM,) * 4,
        scratch_shapes=[
            pltpu.VMEM((4 * block, width), bf16),
            pltpu.VMEM((width // PAIR, 4 * block, 2 * PAIR), bf16),
        ],
        compiler_params=LIMIT,
        cost_estimate=pl.CostEstimate(flops=4_000_000_000, bytes_accessed=4_000_000, transcendentals=2_000_000),
        name="early",
    )(early_bias, query, keys, values, kept_before, kept_after, other, spatial_qkv)
    hidden = pl.pallas_call(
        late_kernel,
        out_shape=pltpu.HBM((rows, width), bf16),
        in_specs=[VMEM] * 11,
        out_specs=HBM,
        scratch_shapes=[
            pltpu.VMEM((rows, width), bf16),
            pltpu.VMEM((width // PAIR, rows, 2 * PAIR), bf16),
            pltpu.VMEM((rows, width), bf16),
            pltpu.VMEM((rows, width), bf16),
            pltpu.SemaphoreType.DMA,
        ],
        compiler_params=LIMIT,
        name="late",
    )(
        late_bias, query, sums, tops, totals, other_before, other_after,
        base, other, spatial_qkv, spatial_out,
    )

    group = rows // members
    hidden = lax.all_to_all(hidden.reshape(members, group, width), COLUMN, 0, 0, tiled=True)

    layer = pl.pallas_call(
        time_kernel,
        out_shape=pltpu.HBM((rows, width), bf16),
        in_specs=[VMEM] * 5,
        out_specs=HBM,
        scratch_shapes=[
            pltpu.VMEM((width // PAIR, 2 * rows, PAIR), bf16),
            pltpu.VMEM((rows, width), bf16),
            pltpu.VMEM((width // PAIR, rows, 2 * PAIR), bf16),
            pltpu.VMEM((rows, width), bf16),
            pltpu.VMEM((rows, width), bf16),
            pltpu.SemaphoreType.DMA,
        ],
        compiler_params=LIMIT,
        name="temporal",
    )(hidden.reshape(rows, width), cosine, sine, time_qkv, time_out)
    return lax.all_to_all(
        layer.reshape(members, group, width), ("chip", "core"), 0, 1, tiled=True
    )


def solution(mesh):
    res, frame = mesh.devices.shape
    fine = Mesh(mesh.devices.reshape(res // 2, 2, frame // 2, 2), ("pair", "half", "chip", "core"))
    placed = (P(("chip", "core"), ("pair", "half"), None), P(), P(), P(), P(), P(), P())
    return jax.shard_map(
        shards, mesh=fine, in_specs=placed, out_specs=placed[0], check_vma=False
    )
```

```python
import math

import jax
import jax.numpy as jnp
from jax import lax
from jax.experimental import pallas as pl
from jax.experimental.pallas import tpu as pltpu
from jax.sharding import Mesh
from jax.sharding import PartitionSpec as P

HEAD = 64
PAIR = 2 * HEAD
EXCLUDED = -1e30
LOG2E = 1.4426950408889634
SCALE = LOG2E / 8.0
COLUMN = ("half", "chip", "core")
VMEM = pl.BlockSpec(memory_space=pltpu.VMEM)
SMEM = pl.BlockSpec(memory_space=pltpu.SMEM)
HBM = pl.BlockSpec(memory_space=pltpu.HBM)
LIMIT = pltpu.CompilerParams(vmem_limit_bytes=24 * 1024 * 1024)


def unit_rows(rows):
    widened = rows.astype(jnp.float32)
    mean_square = jnp.mean(widened * widened, axis=-1, keepdims=True)
    return (widened * lax.rsqrt(mean_square + 1e-06)).astype(jnp.bfloat16)


def dot(left, right):
    return jnp.dot(left, right, preferred_element_type=jnp.float32)


def dot_rows(left, right):
    return lax.dot_general(
        left, right, (((1,), (1,)), ((), ())), preferred_element_type=jnp.float32
    )


def by_head(pair_query):
    lane = lax.broadcasted_iota(jnp.int32, pair_query.shape, 1)
    nothing = jnp.zeros_like(pair_query)
    return jnp.concatenate(
        [jnp.where(lane < HEAD, pair_query, nothing), jnp.where(lane < HEAD, nothing, pair_query)], axis=0
    )


def side_by_side(stacked):
    rows = stacked.shape[0] // 2
    lane = lax.broadcasted_iota(jnp.int32, (rows, PAIR), 1)
    return jnp.where(lane < HEAD, stacked[:rows, :PAIR], stacked[rows:, :PAIR])


def two_rows(bias_ref, block):
    halves = [jnp.broadcast_to(bias_ref[y : y + 1, :], (block, bias_ref.shape[1])) for y in range(2)]
    return jnp.concatenate(halves * 2, axis=0)


def attend(stacked_query, keys, values, pairs, biases, finish, floors=None):
    width = keys.shape[0]

    def scores_of(pair):
        return dot_rows(stacked_query[pair], keys[:, pair * PAIR : (pair + 1) * PAIR]) + biases

    scores = scores_of(0)
    for pair in range(pairs):
        ahead = scores_of(pair + 1) if pair + 1 < pairs else None
        top = jnp.broadcast_to(jnp.max(scores, axis=-1, keepdims=True), (scores.shape[0], PAIR))
        if floors is not None:
            top = jnp.maximum(top, floors[pair])
        expo = jnp.exp2(scores - jnp.concatenate([top] * (width // PAIR), axis=1)).astype(jnp.bfloat16)
        finish(pair, top, dot(expo, values[pair]))
        scores = ahead


def give_kernel(act_ref, given_ref, semaphore):
    move = pltpu.make_async_copy(act_ref.at[1 - lax.axis_index("half")], given_ref, semaphore)
    move.start()
    move.wait()


def contact_biases(contacts_ref, early_ref, late_ref):
    half, pair = lax.axis_index("half"), lax.axis_index("pair")
    block = early_ref.shape[1] // 4
    to_other = 1 - 2 * half
    for row, (parity, moves) in enumerate(
        (
            (half, (0, -2, 2, to_other, to_other - 2, to_other + 2)),
            (1 - half, (-to_other, -to_other - 2, -to_other + 2, 0, -2, 2)),
        )
    ):
        for tile, move in enumerate(moves):
            column = jnp.clip(move + 2, 0, 4)
            flag = jnp.where(column == move + 2, contacts_ref[2 * pair + parity, column], 0)
            ref, at = (early_ref, tile) if tile < 4 else (late_ref, tile - 4)
            ref[row : row + 1, at * block : (at + 1) * block] = jnp.full(
                (1, block), jnp.where(flag > 0, 0.0, EXCLUDED), jnp.float32
            )


def rotation_tables(frame_ref, cos_ref, sin_ref):
    frames, lanes = cos_ref.shape
    row = lax.broadcasted_iota(jnp.int32, (frames, lanes), 0)
    lane = lax.broadcasted_iota(jnp.int32, (frames, lanes), 1)
    position = jnp.zeros((frames, lanes), jnp.int32)
    for j in range(frames):
        frame = 2 * (j % (frames // 2)) + j // (frames // 2)
        position = jnp.where(row == j, frame_ref[frame], position)
    half_size = HEAD // 2
    exponent = (lane % half_size).astype(jnp.float32) * (-math.log(10000.0) / half_size)
    angles = position.astype(jnp.float32) * jnp.exp(exponent)
    cos_ref[...] = jnp.cos(angles)
    sine = jnp.sin(angles)
    sin_ref[...] = jnp.where(lane % HEAD < half_size, -sine, sine)


def first_kernel(
    contacts_ref, frame_ref, given_ref, act_ref, qkv_hbm, out_hbm, time_qkv_hbm, time_out_hbm,
    qkv_ref, out_ref, time_qkv_ref, time_out_ref, normed_ref, base_ref, query_ref, keys_ref, values_ref,
    early_ref, late_ref, cos_ref, sin_ref, semaphores,
):
    half = lax.axis_index("half")
    width = base_ref.shape[1]
    own = pltpu.make_async_copy(act_ref.at[half], base_ref, semaphores.at[0])
    own.start()
    loads = []
    for at, (source, target) in enumerate(
        ((qkv_hbm, qkv_ref), (out_hbm, out_ref), (time_qkv_hbm, time_qkv_ref), (time_out_hbm, time_out_ref))
    ):
        loads.append(pltpu.make_async_copy(source, target, semaphores.at[at + 1]))
        loads[-1].start()
    own.wait()
    normed = unit_rows(base_ref[...])
    normed_ref[...] = normed
    loads[0].wait()
    query_ref[...] = (dot(normed, qkv_ref[:, :width]) * SCALE).astype(jnp.bfloat16)
    keys_ref[...] = dot(normed, qkv_ref[:, width : 2 * width]).astype(jnp.bfloat16)
    values_ref[...] = dot(normed, qkv_ref[:, 2 * width :]).astype(jnp.bfloat16)
    contact_biases(contacts_ref, early_ref, late_ref)
    rotation_tables(frame_ref, cos_ref, sin_ref)
    for load in loads[1:]:
        load.wait()


def early_kernel(
    bias_ref, query_in, keys_in, values_in, before_ref, after_ref, other_ref, qkv_ref,
    query_ref, sums_ref, tops_ref, totals_ref, keys, values,
):
    block, width = other_ref.shape
    pairs = width // PAIR
    normed = unit_rows(other_ref[...])
    query = (dot(normed, qkv_ref[:, :width]) * SCALE).astype(jnp.bfloat16)
    keys[:block, :] = keys_in[...]
    tiles = jnp.concatenate([before_ref[...], after_ref[...], normed], axis=0)
    keys[block:, :] = dot(tiles, qkv_ref[:, width : 2 * width]).astype(jnp.bfloat16)
    fresh = dot(tiles, qkv_ref[:, 2 * width :]).astype(jnp.bfloat16)
    for pair in range(pairs):
        at = slice(pair * PAIR, (pair + 1) * PAIR)
        values[pair, :block, :PAIR] = values_in[:, at]
        values[pair, block:, :PAIR] = fresh[:, at]
        values[pair, :, PAIR:] = jnp.ones((4 * block, PAIR), jnp.bfloat16)
        query_ref[pair] = by_head(jnp.concatenate([query_in[:, at], query[:, at]], axis=0))

    def finish(pair, top, product):
        at = slice(pair * PAIR, (pair + 1) * PAIR)
        tops_ref[pair] = top
        sums_ref[:, at] = side_by_side(product)
        totals_ref[:, at] = side_by_side(product[:, PAIR:])

    attend(query_ref, keys, values, pairs, two_rows(bias_ref, block), finish)


def late_kernel(
    bias_ref, query_ref, sums_ref, tops_ref, totals_ref, before_ref, after_ref,
    base_ref, other_ref, qkv_ref, out_ref, hidden_ref, keys, values, mix,
):
    half = lax.axis_index("half")
    block, width = other_ref.shape
    pairs = width // PAIR
    tiles = unit_rows(jnp.concatenate([before_ref[...], after_ref[...]], axis=0))
    keys[...] = dot(tiles, qkv_ref[:, width : 2 * width]).astype(jnp.bfloat16)
    fresh = dot(tiles, qkv_ref[:, 2 * width :]).astype(jnp.bfloat16)
    for pair in range(pairs):
        values[pair, :, :PAIR] = fresh[:, pair * PAIR : (pair + 1) * PAIR]
        values[pair, :, PAIR:] = jnp.ones((2 * block, PAIR), jnp.bfloat16)

    def finish(pair, top, product):
        at = slice(pair * PAIR, (pair + 1) * PAIR)
        share = side_by_side(jnp.exp2(tops_ref[pair] - top))
        total = totals_ref[:, at] * share + side_by_side(product[:, PAIR:])
        mix[:, at] = ((sums_ref[:, at] * share + side_by_side(product)) / total).astype(jnp.bfloat16)

    attend(query_ref, keys, values, pairs, two_rows(bias_ref, block), finish, tops_ref)
    added = dot(mix[...], out_ref[...])
    here = pl.ds(pl.multiple_of(half * block, block), block)
    there = pl.ds(pl.multiple_of((1 - half) * block, block), block)
    hidden_ref[here, :] = (base_ref[...].astype(jnp.float32) + added[:block]).astype(jnp.bfloat16)
    hidden_ref[there, :] = (other_ref[...].astype(jnp.float32) + added[block:]).astype(jnp.bfloat16)


def time_kernel(
    hidden_ref, cos_ref, sin_ref, qkv_ref, out_w_ref, layer_ref, query, keys, values, mix
):
    rows, width = hidden_ref.shape
    frames = cos_ref.shape[0]
    group = rows // frames
    normed = unit_rows(hidden_ref[...])
    cosine = jnp.concatenate(
        [jnp.broadcast_to(cos_ref[f : f + 1, :], (group, PAIR)) for f in range(frames)], axis=0
    )
    sine = jnp.concatenate(
        [jnp.broadcast_to(sin_ref[f : f + 1, :], (group, PAIR)) for f in range(frames)], axis=0
    )
    source = lax.broadcasted_iota(jnp.int32, (PAIR, PAIR), 0)
    target = lax.broadcasted_iota(jnp.int32, (PAIR, PAIR), 1)
    exchange = jnp.where(source == target ^ (HEAD // 2), 1.0, 0.0).astype(jnp.bfloat16)

    def rotate(entries):
        entries = entries.astype(jnp.bfloat16)
        return entries.astype(jnp.float32) * cosine + dot(entries, exchange) * sine

    pairs = width // PAIR
    projected = dot(normed, qkv_ref[...])
    for pair in range(pairs):
        at = slice(pair * PAIR, (pair + 1) * PAIR)
        query[pair] = by_head((rotate(projected[:, at]) * SCALE).astype(jnp.bfloat16))
        keys[:, at] = rotate(projected[:, width + pair * PAIR : width + (pair + 1) * PAIR]).astype(jnp.bfloat16)
        values[pair, :, :PAIR] = projected[:, 2 * width + pair * PAIR : 2 * width + (pair + 1) * PAIR].astype(jnp.bfloat16)
        values[pair, :, PAIR:] = jnp.ones((rows, PAIR), jnp.bfloat16)
    row = lax.broadcasted_iota(jnp.int32, (2 * rows, rows), 0)
    column = lax.broadcasted_iota(jnp.int32, (2 * rows, rows), 1)
    biases = jnp.where(row % group == column % group, 0.0, EXCLUDED)

    def finish(pair, top, product):
        mixed = side_by_side(product) / side_by_side(product[:, PAIR:])
        mix[:, pair * PAIR : (pair + 1) * PAIR] = mixed.astype(jnp.bfloat16)

    attend(query, keys, values, pairs, biases, finish)
    added = (hidden_ref[...].astype(jnp.float32) + dot(mix[...], out_w_ref[...])).astype(jnp.bfloat16)
    per_half = frames // 2
    for j in range(frames):
        frame = 2 * (j % per_half) + j // per_half
        layer_ref[frame * group : (frame + 1) * group, :] = added[j * group : (j + 1) * group, :]


def shards(activations, contacts, frame_index, spatial_qkv, spatial_out, time_qkv, time_out):
    frames_dev, block, width = activations.shape
    pairs = lax.axis_size("pair")
    activations, spatial_qkv, spatial_out, time_qkv, time_out = (
        pltpu.with_memory_space_constraint(x, pltpu.HBM)
        for x in (activations, spatial_qkv, spatial_out, time_qkv, time_out)
    )
    rows = 2 * block
    bf16, f32 = jnp.bfloat16, jnp.float32
    given = pl.pallas_call(
        give_kernel,
        out_shape=pltpu.VMEM((block, width), bf16),
        in_specs=[HBM],
        out_specs=VMEM,
        scratch_shapes=[pltpu.SemaphoreType.DMA],
        name="give",
    )(activations)
    other = lax.ppermute(given, "half", [(0, 1), (1, 0)])

    def from_neighbours(tile):
        before = lax.ppermute(tile, "pair", [(i, (i + 1) % pairs) for i in range(pairs)])
        after = lax.ppermute(tile, "pair", [((i + 1) % pairs, i) for i in range(pairs)])
        return before, after

    tile_in_vmem = pltpu.VMEM((block, width), bf16)
    weights = (spatial_qkv, spatial_out, time_qkv, time_out)
    members = 2 * lax.axis_size("chip") * lax.axis_size("core")
    table = pltpu.VMEM((members, PAIR), f32)
    *weights, normed, base, query, keys, values, early_bias, late_bias, cosine, sine = pl.pallas_call(
        first_kernel,
        out_shape=tuple(pltpu.VMEM(w.shape, bf16) for w in weights)
        + (tile_in_vmem,)
        + (tile_in_vmem,) * 4
        + (pltpu.VMEM((2, 4 * block), f32), pltpu.VMEM((2, 2 * block), f32), table, table),
        in_specs=[SMEM] * 2 + [VMEM] + [HBM] * 5,
        out_specs=(VMEM,) * 13,
        scratch_shapes=[pltpu.SemaphoreType.DMA((5,))],
        compiler_params=LIMIT,
        cost_estimate=pl.CostEstimate(flops=2 * block * width * 3 * width, bytes_accessed=10_000_000, transcendentals=0),
        name="first",
    )(contacts, frame_index, given, activations, *weights)
    spatial_qkv, spatial_out, time_qkv, time_out = weights
    kept_before, kept_after = from_neighbours(normed)
    other_before, other_after = from_neighbours(other)

    wide = pltpu.VMEM((rows, width), f32)
    tops_shape = pltpu.VMEM((width // PAIR, 2 * rows, PAIR), f32)
    query, sums, tops, totals = pl.pallas_call(
        early_kernel,
        out_shape=(pltpu.VMEM((width // PAIR, 2 * rows, PAIR), bf16), wide, tops_shape, wide),
        in_specs=[VMEM] * 8,
        out_specs=(VMEM,) * 4,
        scratch_shapes=[
            pltpu.VMEM((4 * block, width), bf16),
            pltpu.VMEM((width // PAIR, 4 * block, 2 * PAIR), bf16),
        ],
        compiler_params=LIMIT,
        cost_estimate=pl.CostEstimate(flops=4_000_000_000, bytes_accessed=4_000_000, transcendentals=2_000_000),
        name="early",
    )(early_bias, query, keys, values, kept_before, kept_after, other, spatial_qkv)
    hidden = pl.pallas_call(
        late_kernel,
        out_shape=pltpu.VMEM((rows, width), bf16),
        in_specs=[VMEM] * 11,
        out_specs=VMEM,
        scratch_shapes=[
            pltpu.VMEM((rows, width), bf16),
            pltpu.VMEM((width // PAIR, rows, 2 * PAIR), bf16),
            pltpu.VMEM((rows, width), bf16),
        ],
        compiler_params=LIMIT,
        name="late",
    )(
        late_bias, query, sums, tops, totals, other_before, other_after,
        base, other, spatial_qkv, spatial_out,
    )

    group = rows // members
    hidden = lax.all_to_all(hidden.reshape(members, group, width), COLUMN, 0, 0, tiled=True)

    layer = pl.pallas_call(
        time_kernel,
        out_shape=pltpu.VMEM((rows, width), bf16),
        in_specs=[VMEM] * 5,
        out_specs=VMEM,
        scratch_shapes=[
            pltpu.VMEM((width // PAIR, 2 * rows, PAIR), bf16),
            pltpu.VMEM((rows, width), bf16),
            pltpu.VMEM((width // PAIR, rows, 2 * PAIR), bf16),
            pltpu.VMEM((rows, width), bf16),
        ],
        compiler_params=LIMIT,
        name="temporal",
    )(hidden.reshape(rows, width), cosine, sine, time_qkv, time_out)
    return lax.all_to_all(
        layer.reshape(members, group, width), ("chip", "core"), 0, 1, tiled=True
    )


def solution(mesh):
    res, frame = mesh.devices.shape
    fine = Mesh(mesh.devices.reshape(res // 2, 2, frame // 2, 2), ("pair", "half", "chip", "core"))
    placed = (P(("chip", "core"), ("pair", "half"), None), P(), P(), P(), P(), P(), P())
    return jax.shard_map(
        shards, mesh=fine, in_specs=placed, out_specs=placed[0], check_vma=False
    )
```

```python
import math

import jax
import jax.numpy as jnp
from jax import lax
from jax.experimental import pallas as pl
from jax.experimental.pallas import tpu as pltpu
from jax.sharding import Mesh
from jax.sharding import PartitionSpec as P

HEAD = 64
PAIR = 2 * HEAD
EXCLUDED = -1e30
LOG2E = 1.4426950408889634
SCALE = LOG2E / 8.0
COLUMN = ("half", "chip", "core")
VMEM = pl.BlockSpec(memory_space=pltpu.VMEM)
SMEM = pl.BlockSpec(memory_space=pltpu.SMEM)
HBM = pl.BlockSpec(memory_space=pltpu.HBM)
LIMIT = pltpu.CompilerParams(vmem_limit_bytes=24 * 1024 * 1024)


def unit_rows(rows):
    widened = rows.astype(jnp.float32)
    mean_square = jnp.mean(widened * widened, axis=-1, keepdims=True)
    return (widened * lax.rsqrt(mean_square + 1e-06)).astype(jnp.bfloat16)


def dot(left, right):
    return jnp.dot(left, right, preferred_element_type=jnp.float32)


def dot_rows(left, right):
    return lax.dot_general(
        left, right, (((1,), (1,)), ((), ())), preferred_element_type=jnp.float32
    )


def by_head(pair_query):
    lane = lax.broadcasted_iota(jnp.int32, pair_query.shape, 1)
    nothing = jnp.zeros_like(pair_query)
    return jnp.concatenate(
        [jnp.where(lane < HEAD, pair_query, nothing), jnp.where(lane < HEAD, nothing, pair_query)], axis=0
    )


def side_by_side(stacked):
    rows = stacked.shape[0] // 2
    lane = lax.broadcasted_iota(jnp.int32, (rows, PAIR), 1)
    return jnp.where(lane < HEAD, stacked[:rows, :PAIR], stacked[rows:, :PAIR])


def two_rows(bias_ref, block):
    halves = [jnp.broadcast_to(bias_ref[y : y + 1, :], (block, bias_ref.shape[1])) for y in range(2)]
    return jnp.concatenate(halves * 2, axis=0)


def attend(stacked_query, keys, values, pairs, biases, finish, floors=None):
    width = keys.shape[0]

    def scores_of(pair):
        return dot_rows(stacked_query[pair], keys[:, pair * PAIR : (pair + 1) * PAIR]) + biases

    scores = scores_of(0)
    for pair in range(pairs):
        ahead = scores_of(pair + 1) if pair + 1 < pairs else None
        top = jnp.broadcast_to(jnp.max(scores, axis=-1, keepdims=True), (scores.shape[0], PAIR))
        if floors is not None:
            top = jnp.maximum(top, floors[pair])
        expo = jnp.exp2(scores - jnp.concatenate([top] * (width // PAIR), axis=1)).astype(jnp.bfloat16)
        finish(pair, top, dot(expo, values[pair]))
        scores = ahead


def give_kernel(act_ref, given_ref, semaphore):
    move = pltpu.make_async_copy(act_ref.at[1 - lax.axis_index("half")], given_ref, semaphore)
    move.start()
    move.wait()


def contact_biases(contacts_ref, early_ref, late_ref):
    half, pair = lax.axis_index("half"), lax.axis_index("pair")
    block = early_ref.shape[1] // 4
    to_other = 1 - 2 * half
    odd = 4 * (pair % 2) - 2
    for row, (parity, moves) in enumerate(
        (
            (half, (0, odd, -odd, to_other, to_other + odd, to_other - odd)),
            (1 - half, (-to_other, odd - to_other, -odd - to_other, 0, odd, -odd)),
        )
    ):
        for tile, move in enumerate(moves):
            column = jnp.clip(move + 2, 0, 4)
            flag = jnp.where(column == move + 2, contacts_ref[column, 2 * pair + parity], 0)
            ref, at = (early_ref, tile) if tile < 4 else (late_ref, tile - 4)
            ref[row : row + 1, at * block : (at + 1) * block] = jnp.full(
                (1, block), jnp.where(flag > 0, 0.0, EXCLUDED), jnp.float32
            )


def rotation_tables(frame_ref, cos_ref, sin_ref):
    frames, lanes = cos_ref.shape
    row = lax.broadcasted_iota(jnp.int32, (frames, lanes), 0)
    lane = lax.broadcasted_iota(jnp.int32, (frames, lanes), 1)
    position = jnp.zeros((frames, lanes), jnp.int32)
    for j in range(frames):
        frame = 2 * (j % (frames // 2)) + j // (frames // 2)
        position = jnp.where(row == j, frame_ref[frame], position)
    half_size = HEAD // 2
    exponent = (lane % half_size).astype(jnp.float32) * (-math.log(10000.0) / half_size)
    angles = position.astype(jnp.float32) * jnp.exp(exponent)
    cos_ref[...] = jnp.cos(angles)
    sine = jnp.sin(angles)
    sin_ref[...] = jnp.where(lane % HEAD < half_size, -sine, sine)


def first_kernel(
    contacts_hbm, frame_hbm, given_ref, act_ref, qkv_hbm,
    qkv_ref, normed_ref, base_ref, query_ref, keys_ref, values_ref, early_ref, late_ref, cos_ref, sin_ref,
    contacts_ref, frame_ref, semaphores,
):
    half = lax.axis_index("half")
    width = base_ref.shape[1]
    own = pltpu.make_async_copy(act_ref.at[half], base_ref, semaphores.at[0])
    own.start()
    loads = [
        pltpu.make_async_copy(source, target, semaphores.at[at + 1])
        for at, (source, target) in enumerate(
            ((qkv_hbm, qkv_ref), (contacts_hbm, contacts_ref), (frame_hbm, frame_ref))
        )
    ]
    for load in loads:
        load.start()
    own.wait()
    normed = unit_rows(base_ref[...])
    normed_ref[...] = normed
    loads[0].wait()
    query_ref[...] = (dot(normed, qkv_ref[:, :width]) * SCALE).astype(jnp.bfloat16)
    keys_ref[...] = dot(normed, qkv_ref[:, width : 2 * width]).astype(jnp.bfloat16)
    values_ref[...] = dot(normed, qkv_ref[:, 2 * width :]).astype(jnp.bfloat16)
    for load in loads[1:]:
        load.wait()
    contact_biases(contacts_ref, early_ref, late_ref)
    rotation_tables(frame_ref, cos_ref, sin_ref)


def early_kernel(
    bias_ref, query_in, keys_in, values_in, odd_ref, even_ref, other_ref, qkv_ref, out_hbm, time_qkv_hbm,
    time_out_hbm, query_ref, sums_ref, tops_ref, totals_ref, out_ref, time_qkv_ref, time_out_ref,
    keys, values, semaphores,
):
    loads = [
        pltpu.make_async_copy(source, target, semaphores.at[at])
        for at, (source, target) in enumerate(
            ((out_hbm, out_ref), (time_qkv_hbm, time_qkv_ref), (time_out_hbm, time_out_ref))
        )
    ]
    for load in loads:
        load.start()
    block, width = other_ref.shape
    pairs = width // PAIR
    normed = unit_rows(other_ref[...])
    query = (dot(normed, qkv_ref[:, :width]) * SCALE).astype(jnp.bfloat16)
    keys[:block, :] = keys_in[...]
    tiles = jnp.concatenate([odd_ref[...], even_ref[...], normed], axis=0)
    keys[block:, :] = dot(tiles, qkv_ref[:, width : 2 * width]).astype(jnp.bfloat16)
    fresh = dot(tiles, qkv_ref[:, 2 * width :]).astype(jnp.bfloat16)
    for pair in range(pairs):
        at = slice(pair * PAIR, (pair + 1) * PAIR)
        values[pair, :block, :PAIR] = values_in[:, at]
        values[pair, block:, :PAIR] = fresh[:, at]
        values[pair, :, PAIR:] = jnp.ones((4 * block, PAIR), jnp.bfloat16)
        query_ref[pair] = by_head(jnp.concatenate([query_in[:, at], query[:, at]], axis=0))

    def finish(pair, top, product):
        at = slice(pair * PAIR, (pair + 1) * PAIR)
        tops_ref[pair] = top
        sums_ref[:, at] = side_by_side(product)
        totals_ref[:, at] = side_by_side(product[:, PAIR:])

    attend(query_ref, keys, values, pairs, two_rows(bias_ref, block), finish)
    for load in loads:
        load.wait()


def late_kernel(
    bias_ref, query_ref, sums_ref, tops_ref, totals_ref, odd_ref, even_ref,
    base_ref, other_ref, qkv_ref, out_ref, hidden_ref, keys, values, mix,
):
    half = lax.axis_index("half")
    block, width = other_ref.shape
    pairs = width // PAIR
    tiles = unit_rows(jnp.concatenate([odd_ref[...], even_ref[...]], axis=0))
    keys[...] = dot(tiles, qkv_ref[:, width : 2 * width]).astype(jnp.bfloat16)
    fresh = dot(tiles, qkv_ref[:, 2 * width :]).astype(jnp.bfloat16)
    for pair in range(pairs):
        values[pair, :, :PAIR] = fresh[:, pair * PAIR : (pair + 1) * PAIR]
        values[pair, :, PAIR:] = jnp.ones((2 * block, PAIR), jnp.bfloat16)

    def finish(pair, top, product):
        at = slice(pair * PAIR, (pair + 1) * PAIR)
        share = side_by_side(jnp.exp2(tops_ref[pair] - top))
        total = totals_ref[:, at] * share + side_by_side(product[:, PAIR:])
        mix[:, at] = ((sums_ref[:, at] * share + side_by_side(product)) / total).astype(jnp.bfloat16)

    attend(query_ref, keys, values, pairs, two_rows(bias_ref, block), finish, tops_ref)
    added = dot(mix[...], out_ref[...])
    here = pl.ds(pl.multiple_of(half * block, block), block)
    there = pl.ds(pl.multiple_of((1 - half) * block, block), block)
    hidden_ref[here, :] = (base_ref[...].astype(jnp.float32) + added[:block]).astype(jnp.bfloat16)
    hidden_ref[there, :] = (other_ref[...].astype(jnp.float32) + added[block:]).astype(jnp.bfloat16)


def time_kernel(
    hidden_ref, cos_ref, sin_ref, qkv_ref, out_w_ref, layer_ref, query, keys, values, mix
):
    rows, width = hidden_ref.shape
    frames = cos_ref.shape[0]
    group = rows // frames
    normed = unit_rows(hidden_ref[...])
    cosine = jnp.concatenate(
        [jnp.broadcast_to(cos_ref[f : f + 1, :], (group, PAIR)) for f in range(frames)], axis=0
    )
    sine = jnp.concatenate(
        [jnp.broadcast_to(sin_ref[f : f + 1, :], (group, PAIR)) for f in range(frames)], axis=0
    )
    source = lax.broadcasted_iota(jnp.int32, (PAIR, PAIR), 0)
    target = lax.broadcasted_iota(jnp.int32, (PAIR, PAIR), 1)
    exchange = jnp.where(source == target ^ (HEAD // 2), 1.0, 0.0).astype(jnp.bfloat16)

    def rotate(entries):
        entries = entries.astype(jnp.bfloat16)
        return entries.astype(jnp.float32) * cosine + dot(entries, exchange) * sine

    pairs = width // PAIR
    projected = dot(normed, qkv_ref[...])
    for pair in range(pairs):
        at = slice(pair * PAIR, (pair + 1) * PAIR)
        query[pair] = by_head((rotate(projected[:, at]) * SCALE).astype(jnp.bfloat16))
        keys[:, at] = rotate(projected[:, width + pair * PAIR : width + (pair + 1) * PAIR]).astype(jnp.bfloat16)
        values[pair, :, :PAIR] = projected[:, 2 * width + pair * PAIR : 2 * width + (pair + 1) * PAIR].astype(jnp.bfloat16)
        values[pair, :, PAIR:] = jnp.ones((rows, PAIR), jnp.bfloat16)
    row = lax.broadcasted_iota(jnp.int32, (2 * rows, rows), 0)
    column = lax.broadcasted_iota(jnp.int32, (2 * rows, rows), 1)
    biases = jnp.where(row % group == column % group, 0.0, EXCLUDED)

    def finish(pair, top, product):
        mixed = side_by_side(product) / side_by_side(product[:, PAIR:])
        mix[:, pair * PAIR : (pair + 1) * PAIR] = mixed.astype(jnp.bfloat16)

    attend(query, keys, values, pairs, biases, finish)
    added = (hidden_ref[...].astype(jnp.float32) + dot(mix[...], out_w_ref[...])).astype(jnp.bfloat16)
    per_half = frames // 2
    for j in range(frames):
        frame = 2 * (j % per_half) + j // per_half
        layer_ref[frame * group : (frame + 1) * group, :] = added[j * group : (j + 1) * group, :]


def shards(activations, contacts, frame_index, spatial_qkv, spatial_out, time_qkv, time_out):
    frames_dev, block, width = activations.shape
    pairs = lax.axis_size("pair")
    activations, spatial_qkv, spatial_out, time_qkv, time_out = (
        pltpu.with_memory_space_constraint(x, pltpu.HBM)
        for x in (activations, spatial_qkv, spatial_out, time_qkv, time_out)
    )
    rows = 2 * block
    bf16, f32 = jnp.bfloat16, jnp.float32
    given = pl.pallas_call(
        give_kernel,
        out_shape=pltpu.VMEM((block, width), bf16),
        in_specs=[HBM],
        out_specs=VMEM,
        scratch_shapes=[pltpu.SemaphoreType.DMA],
        name="give",
    )(activations)
    other = lax.ppermute(given, "half", [(0, 1), (1, 0)])

    column = lax.axis_size("half") * lax.axis_size("chip") * lax.axis_size("core")
    even, odd = [], []
    for i in range(pairs):
        for place in range(column):
            at = i * column + place
            even.append((at, (i ^ 1) * column + place))
            if i in (0, pairs - 1):
                odd.append((at, at ^ 1))
            else:
                odd.append((at, (((i - 1) ^ 1) + 1) * column + place))

    def from_neighbours(tile):
        axes = ("pair",) + COLUMN
        return lax.ppermute(tile, axes, odd), lax.ppermute(tile, axes, even)

    tile_in_vmem = pltpu.VMEM((block, width), bf16)
    members = 2 * lax.axis_size("chip") * lax.axis_size("core")
    table = pltpu.VMEM((members, PAIR), f32)
    by_offset = contacts.T
    spatial_qkv, normed, base, query, keys, values, early_bias, late_bias, cosine, sine = pl.pallas_call(
        first_kernel,
        out_shape=(pltpu.VMEM(spatial_qkv.shape, bf16),)
        + (tile_in_vmem,) * 5
        + (pltpu.VMEM((2, 4 * block), f32), pltpu.VMEM((2, 2 * block), f32), table, table),
        in_specs=[HBM] * 2 + [VMEM] + [HBM] * 2,
        out_specs=(VMEM,) * 10,
        scratch_shapes=[
            pltpu.SMEM(by_offset.shape, jnp.int32),
            pltpu.SMEM(frame_index.shape, jnp.int32),
            pltpu.SemaphoreType.DMA((4,)),
        ],
        compiler_params=LIMIT,
        cost_estimate=pl.CostEstimate(flops=2 * block * width * 3 * width, bytes_accessed=4_000_000, transcendentals=0),
        name="first",
    )(
        pltpu.with_memory_space_constraint(by_offset, pltpu.HBM),
        pltpu.with_memory_space_constraint(frame_index, pltpu.HBM),
        given, activations, spatial_qkv,
    )
    kept_odd, kept_even = from_neighbours(normed)
    other_odd, other_even = from_neighbours(other)

    wide = pltpu.VMEM((rows, width), f32)
    tops_shape = pltpu.VMEM((width // PAIR, 2 * rows, PAIR), f32)
    later = (spatial_out, time_qkv, time_out)
    query, sums, tops, totals, spatial_out, time_qkv, time_out = pl.pallas_call(
        early_kernel,
        out_shape=(pltpu.VMEM((width // PAIR, 2 * rows, PAIR), bf16), wide, tops_shape, wide)
        + tuple(pltpu.VMEM(weight.shape, bf16) for weight in later),
        in_specs=[VMEM] * 8 + [HBM] * 3,
        out_specs=(VMEM,) * 7,
        scratch_shapes=[
            pltpu.VMEM((4 * block, width), bf16),
            pltpu.VMEM((width // PAIR, 4 * block, 2 * PAIR), bf16),
            pltpu.SemaphoreType.DMA((3,)),
        ],
        compiler_params=LIMIT,
        cost_estimate=pl.CostEstimate(flops=4_000_000_000, bytes_accessed=4_000_000, transcendentals=2_000_000),
        name="early",
    )(early_bias, query, keys, values, kept_odd, kept_even, other, spatial_qkv, *later)
    hidden = pl.pallas_call(
        late_kernel,
        out_shape=pltpu.VMEM((rows, width), bf16),
        in_specs=[VMEM] * 11,
        out_specs=VMEM,
        scratch_shapes=[
            pltpu.VMEM((rows, width), bf16),
            pltpu.VMEM((width // PAIR, rows, 2 * PAIR), bf16),
            pltpu.VMEM((rows, width), bf16),
        ],
        compiler_params=LIMIT,
        name="late",
    )(
        late_bias, query, sums, tops, totals, other_odd, other_even,
        base, other, spatial_qkv, spatial_out,
    )

    group = rows // members
    hidden = lax.all_to_all(hidden.reshape(members, group, width), COLUMN, 0, 0, tiled=True)

    layer = pl.pallas_call(
        time_kernel,
        out_shape=pltpu.VMEM((rows, width), bf16),
        in_specs=[VMEM] * 5,
        out_specs=VMEM,
        scratch_shapes=[
            pltpu.VMEM((width // PAIR, 2 * rows, PAIR), bf16),
            pltpu.VMEM((rows, width), bf16),
            pltpu.VMEM((width // PAIR, rows, 2 * PAIR), bf16),
            pltpu.VMEM((rows, width), bf16),
        ],
        compiler_params=LIMIT,
        name="temporal",
    )(hidden.reshape(rows, width), cosine, sine, time_qkv, time_out)
    return lax.all_to_all(
        layer.reshape(members, group, width), ("chip", "core"), 0, 1, tiled=True
    )


def solution(mesh):
    res, frame = mesh.devices.shape
    fine = Mesh(mesh.devices.reshape(res // 2, 2, frame // 2, 2), ("pair", "half", "chip", "core"))
    placed = (P(("chip", "core"), ("pair", "half"), None), P(), P(), P(), P(), P(), P())
    return jax.shard_map(
        shards, mesh=fine, in_specs=placed, out_specs=placed[0], check_vma=False
    )
```

```python
import math

import jax
import jax.numpy as jnp
from jax import lax
from jax.experimental import pallas as pl
from jax.experimental.pallas import tpu as pltpu
from jax.sharding import Mesh
from jax.sharding import PartitionSpec as P

HEAD = 64
PAIR = 2 * HEAD
EXCLUDED = -1e30
LOG2E = 1.4426950408889634
SCALE = LOG2E / 8.0
EXCHANGES = (0, 2, 3, 1)
COLUMN = ("half", "chip", "core")
VMEM = pl.BlockSpec(memory_space=pltpu.VMEM)
SMEM = pl.BlockSpec(memory_space=pltpu.SMEM)
HBM = pl.BlockSpec(memory_space=pltpu.HBM)
SMALL = pltpu.CompilerParams(vmem_limit_bytes=4 * 1024 * 1024)
LIMIT = pltpu.CompilerParams(vmem_limit_bytes=24 * 1024 * 1024)


def unit_rows(rows):
    widened = rows.astype(jnp.float32)
    mean_square = jnp.mean(widened * widened, axis=-1, keepdims=True)
    return (widened * lax.rsqrt(mean_square + 1e-06)).astype(jnp.bfloat16)


def dot(left, right):
    return jnp.dot(left, right, preferred_element_type=jnp.float32)


def dot_rows(left, right):
    return lax.dot_general(
        left, right, (((1,), (1,)), ((), ())), preferred_element_type=jnp.float32
    )


def by_head(pair_query):
    lane = lax.broadcasted_iota(jnp.int32, pair_query.shape, 1)
    nothing = jnp.zeros_like(pair_query)
    return jnp.concatenate(
        [jnp.where(lane < HEAD, pair_query, nothing), jnp.where(lane < HEAD, nothing, pair_query)], axis=0
    )


def side_by_side(stacked):
    rows = stacked.shape[0] // 2
    lane = lax.broadcasted_iota(jnp.int32, (rows, PAIR), 1)
    return jnp.where(lane < HEAD, stacked[:rows, :PAIR], stacked[rows:, :PAIR])


def two_rows(bias_ref, block):
    halves = [jnp.broadcast_to(bias_ref[y : y + 1, :], (block, bias_ref.shape[1])) for y in range(2)]
    return jnp.concatenate(halves * 2, axis=0)


def attend(stacked_query, keys, values, pairs, biases, finish, floors=None):
    width = keys.shape[0]

    def scores_of(pair):
        return dot_rows(stacked_query[pair], keys[:, pair * PAIR : (pair + 1) * PAIR]) + biases

    scores = scores_of(0)
    for pair in range(pairs):
        ahead = scores_of(pair + 1) if pair + 1 < pairs else None
        top = jnp.broadcast_to(jnp.max(scores, axis=-1, keepdims=True), (scores.shape[0], PAIR))
        if floors is not None:
            top = jnp.maximum(top, floors[pair])
        expo = jnp.exp2(scores - jnp.concatenate([top] * (width // PAIR), axis=1)).astype(jnp.bfloat16)
        finish(pair, top, dot(expo, values[pair]))
        scores = ahead


def give_kernel(act_ref, given_ref, semaphore):
    move = pltpu.make_async_copy(act_ref.at[1 - lax.axis_index("half")], given_ref, semaphore)
    move.start()
    move.wait()


def contact_biases(contacts_ref, early_ref, late_ref):
    half, pair = lax.axis_index("half"), lax.axis_index("pair")
    block = early_ref.shape[1] // 4
    to_other = 1 - 2 * half
    odd = 4 * (pair % 2) - 2
    for row, (parity, moves) in enumerate(
        (
            (half, (0, odd, -odd, to_other, to_other + odd, to_other - odd)),
            (1 - half, (-to_other, odd - to_other, -odd - to_other, 0, odd, -odd)),
        )
    ):
        for tile, move in enumerate(moves):
            column = jnp.clip(move + 2, 0, 4)
            flag = jnp.where(column == move + 2, contacts_ref[column, 2 * pair + parity], 0)
            ref, at = (early_ref, tile) if tile < 4 else (late_ref, tile - 4)
            ref[row : row + 1, at * block : (at + 1) * block] = jnp.full(
                (1, block), jnp.where(flag > 0, 0.0, EXCLUDED), jnp.float32
            )


def rotation_tables(frame_ref, cos_ref, sin_ref):
    frames, lanes = cos_ref.shape
    row = lax.broadcasted_iota(jnp.int32, (frames, lanes), 0)
    lane = lax.broadcasted_iota(jnp.int32, (frames, lanes), 1)
    position = jnp.zeros((frames, lanes), jnp.int32)
    for j in range(frames):
        frame = 2 * (j % (frames // 2)) + j // (frames // 2)
        position = jnp.where(row == j, frame_ref[frame], position)
    half_size = HEAD // 2
    exponent = (lane % half_size).astype(jnp.float32) * (-math.log(10000.0) / half_size)
    angles = position.astype(jnp.float32) * jnp.exp(exponent)
    cos_ref[...] = jnp.cos(angles)
    sine = jnp.sin(angles)
    sin_ref[...] = jnp.where(lane % HEAD < half_size, -sine, sine)


def first_kernel(
    contacts_hbm, frame_hbm, given_ref, act_ref, qkv_hbm,
    qkv_ref, normed_ref, base_ref, query_ref, keys_ref, values_ref, early_ref, late_ref, cos_ref, sin_ref,
    contacts_ref, frame_ref, semaphores,
):
    half = lax.axis_index("half")
    width = base_ref.shape[1]
    own = pltpu.make_async_copy(act_ref.at[half], base_ref, semaphores.at[0])
    own.start()
    loads = [
        pltpu.make_async_copy(source, target, semaphores.at[at + 1])
        for at, (source, target) in enumerate(
            ((qkv_hbm, qkv_ref), (contacts_hbm, contacts_ref), (frame_hbm, frame_ref))
        )
    ]
    for load in loads:
        load.start()
    own.wait()
    normed = unit_rows(base_ref[...])
    normed_ref[...] = normed
    loads[0].wait()
    query_ref[...] = (dot(normed, qkv_ref[:, :width]) * SCALE).astype(jnp.bfloat16)
    keys_ref[...] = dot(normed, qkv_ref[:, width : 2 * width]).astype(jnp.bfloat16)
    values_ref[...] = dot(normed, qkv_ref[:, 2 * width :]).astype(jnp.bfloat16)
    for load in loads[1:]:
        load.wait()
    contact_biases(contacts_ref, early_ref, late_ref)
    rotation_tables(frame_ref, cos_ref, sin_ref)


def early_kernel(
    bias_ref, query_in, keys_in, values_in, odd_ref, even_ref, other_ref, qkv_ref, out_hbm, time_qkv_hbm,
    time_out_hbm, query_ref, sums_ref, tops_ref, totals_ref, out_ref, time_qkv_ref, time_out_ref,
    keys, values, semaphores,
):
    loads = [
        pltpu.make_async_copy(source, target, semaphores.at[at])
        for at, (source, target) in enumerate(
            ((out_hbm, out_ref), (time_qkv_hbm, time_qkv_ref), (time_out_hbm, time_out_ref))
        )
    ]
    for load in loads:
        load.start()
    block, width = other_ref.shape
    pairs = width // PAIR
    normed = unit_rows(other_ref[...])
    query = (dot(normed, qkv_ref[:, :width]) * SCALE).astype(jnp.bfloat16)
    keys[:block, :] = keys_in[...]
    tiles = jnp.concatenate([odd_ref[...], even_ref[...], normed], axis=0)
    keys[block:, :] = dot(tiles, qkv_ref[:, width : 2 * width]).astype(jnp.bfloat16)
    fresh = dot(tiles, qkv_ref[:, 2 * width :]).astype(jnp.bfloat16)
    for pair in range(pairs):
        at = slice(pair * PAIR, (pair + 1) * PAIR)
        values[pair, :block, :PAIR] = values_in[:, at]
        values[pair, block:, :PAIR] = fresh[:, at]
        values[pair, :, PAIR:] = jnp.ones((4 * block, PAIR), jnp.bfloat16)
        query_ref[pair] = by_head(jnp.concatenate([query_in[:, at], query[:, at]], axis=0))

    def finish(pair, top, product):
        at = slice(pair * PAIR, (pair + 1) * PAIR)
        tops_ref[pair] = top
        sums_ref[:, at] = side_by_side(product)
        totals_ref[:, at] = side_by_side(product[:, PAIR:])

    attend(query_ref, keys, values, pairs, two_rows(bias_ref, block), finish)
    for load in loads:
        load.wait()


def late_kernel(
    bias_ref, query_ref, sums_ref, tops_ref, totals_ref, odd_ref, even_ref,
    base_ref, other_ref, qkv_ref, out_ref, hidden_ref, keys, values, mix,
):
    half = lax.axis_index("half")
    block, width = other_ref.shape
    pairs = width // PAIR
    tiles = unit_rows(jnp.concatenate([odd_ref[...], even_ref[...]], axis=0))
    keys[...] = dot(tiles, qkv_ref[:, width : 2 * width]).astype(jnp.bfloat16)
    fresh = dot(tiles, qkv_ref[:, 2 * width :]).astype(jnp.bfloat16)
    for pair in range(pairs):
        values[pair, :, :PAIR] = fresh[:, pair * PAIR : (pair + 1) * PAIR]
        values[pair, :, PAIR:] = jnp.ones((2 * block, PAIR), jnp.bfloat16)

    def finish(pair, top, product):
        at = slice(pair * PAIR, (pair + 1) * PAIR)
        share = side_by_side(jnp.exp2(tops_ref[pair] - top))
        total = totals_ref[:, at] * share + side_by_side(product[:, PAIR:])
        mix[:, at] = ((sums_ref[:, at] * share + side_by_side(product)) / total).astype(jnp.bfloat16)

    attend(query_ref, keys, values, pairs, two_rows(bias_ref, block), finish, tops_ref)
    added = dot(mix[...], out_ref[...])
    here = pl.ds(pl.multiple_of(half * block, block), block)
    there = pl.ds(pl.multiple_of((1 - half) * block, block), block)
    hidden_ref[here, :] = (base_ref[...].astype(jnp.float32) + added[:block]).astype(jnp.bfloat16)
    hidden_ref[there, :] = (other_ref[...].astype(jnp.float32) + added[block:]).astype(jnp.bfloat16)


def time_kernel(
    hidden_ref, cos_ref, sin_ref, qkv_ref, out_w_ref, own_ref, partner_ref, query, keys, values, mix, layer
):
    rows, width = hidden_ref.shape
    frames = cos_ref.shape[0]
    group = rows // frames
    normed = unit_rows(hidden_ref[...])
    cosine = jnp.concatenate(
        [jnp.broadcast_to(cos_ref[f : f + 1, :], (group, PAIR)) for f in range(frames)], axis=0
    )
    sine = jnp.concatenate(
        [jnp.broadcast_to(sin_ref[f : f + 1, :], (group, PAIR)) for f in range(frames)], axis=0
    )
    source = lax.broadcasted_iota(jnp.int32, (PAIR, PAIR), 0)
    target = lax.broadcasted_iota(jnp.int32, (PAIR, PAIR), 1)
    exchange = jnp.where(source == target ^ (HEAD // 2), 1.0, 0.0).astype(jnp.bfloat16)

    def rotate(entries):
        entries = entries.astype(jnp.bfloat16)
        return entries.astype(jnp.float32) * cosine + dot(entries, exchange) * sine

    pairs = width // PAIR
    projected = dot(normed, qkv_ref[...])
    for pair in range(pairs):
        at = slice(pair * PAIR, (pair + 1) * PAIR)
        query[pair] = by_head((rotate(projected[:, at]) * SCALE).astype(jnp.bfloat16))
        keys[:, at] = rotate(projected[:, width + pair * PAIR : width + (pair + 1) * PAIR]).astype(jnp.bfloat16)
        values[pair, :, :PAIR] = projected[:, 2 * width + pair * PAIR : 2 * width + (pair + 1) * PAIR].astype(jnp.bfloat16)
        values[pair, :, PAIR:] = jnp.ones((rows, PAIR), jnp.bfloat16)
    row = lax.broadcasted_iota(jnp.int32, (2 * rows, rows), 0)
    column = lax.broadcasted_iota(jnp.int32, (2 * rows, rows), 1)
    biases = jnp.where(row % group == column % group, 0.0, EXCLUDED)

    def finish(pair, top, product):
        mixed = side_by_side(product) / side_by_side(product[:, PAIR:])
        mix[:, pair * PAIR : (pair + 1) * PAIR] = mixed.astype(jnp.bfloat16)

    attend(query, keys, values, pairs, biases, finish)
    added = (hidden_ref[...].astype(jnp.float32) + dot(mix[...], out_w_ref[...])).astype(jnp.bfloat16)
    per_half = frames // 2
    for j in range(frames):
        target = (j % 2) * per_half + (j % per_half) // 2 * 2 + j // per_half
        layer[target * group : (target + 1) * group, :] = added[j * group : (j + 1) * group, :]
    core = lax.axis_index("core")
    own_ref[...] = layer[pl.ds(pl.multiple_of(core * (rows // 2), rows // 2), rows // 2), :]
    partner_ref[...] = layer[pl.ds(pl.multiple_of((1 - core) * (rows // 2), rows // 2), rows // 2), :]


def join_kernel(own_ref, partner_ref, *chunk_refs):
    chip, core = lax.axis_index("chip"), lax.axis_index("core")
    rows = own_ref.shape[0] // len(chunk_refs)
    group = rows // 2
    for d, chunk_ref in zip(EXCHANGES, chunk_refs):
        for frame in range(2):
            at = pl.ds(pl.multiple_of((chip ^ d) * rows + frame * group, group), group)
            here = pl.ds(pl.multiple_of(frame * rows + core * group, group), group)
            there = pl.ds(pl.multiple_of(frame * rows + (1 - core) * group, group), group)
            chunk_ref[here, :] = own_ref[at, :]
            chunk_ref[there, :] = partner_ref[at, :]


def assemble_kernel(*refs):
    *chunk_refs, layer_ref, semaphores = refs
    chip = lax.axis_index("chip")
    rows = chunk_refs[0].shape[0] // 2
    moves = []
    for d, chunk_ref in zip(EXCHANGES, chunk_refs):
        at = pl.ds(pl.multiple_of((chip ^ d) * rows, rows), rows)
        for frame in range(2):
            moves.append(
                pltpu.make_async_copy(
                    chunk_ref.at[pl.ds(frame * rows, rows), :], layer_ref.at[frame, at, :], semaphores.at[2 * d + frame]
                )
            )
            moves[-1].start()
    for move in moves:
        move.wait()


def shards(activations, contacts, frame_index, spatial_qkv, spatial_out, time_qkv, time_out):
    frames_dev, block, width = activations.shape
    pairs = lax.axis_size("pair")
    activations, spatial_qkv, spatial_out, time_qkv, time_out = (
        pltpu.with_memory_space_constraint(x, pltpu.HBM)
        for x in (activations, spatial_qkv, spatial_out, time_qkv, time_out)
    )
    rows = 2 * block
    bf16, f32 = jnp.bfloat16, jnp.float32
    given = pl.pallas_call(
        give_kernel,
        out_shape=pltpu.VMEM((block, width), bf16),
        in_specs=[HBM],
        out_specs=VMEM,
        scratch_shapes=[pltpu.SemaphoreType.DMA],
        name="give",
    )(activations)
    other = lax.ppermute(given, "half", [(0, 1), (1, 0)])

    column = lax.axis_size("half") * lax.axis_size("chip") * lax.axis_size("core")
    even, odd = [], []
    for i in range(pairs):
        for place in range(column):
            at = i * column + place
            even.append((at, (i ^ 1) * column + place))
            if i in (0, pairs - 1):
                odd.append((at, at ^ 1))
            else:
                odd.append((at, (((i - 1) ^ 1) + 1) * column + place))

    def from_neighbours(tile):
        axes = ("pair",) + COLUMN
        return lax.ppermute(tile, axes, odd), lax.ppermute(tile, axes, even)

    tile_in_vmem = pltpu.VMEM((block, width), bf16)
    members = 2 * lax.axis_size("chip") * lax.axis_size("core")
    table = pltpu.VMEM((members, PAIR), f32)
    by_offset = contacts.T
    spatial_qkv, normed, base, query, keys, values, early_bias, late_bias, cosine, sine = pl.pallas_call(
        first_kernel,
        out_shape=(pltpu.VMEM(spatial_qkv.shape, bf16),)
        + (tile_in_vmem,) * 5
        + (pltpu.VMEM((2, 4 * block), f32), pltpu.VMEM((2, 2 * block), f32), table, table),
        in_specs=[HBM] * 2 + [VMEM] + [HBM] * 2,
        out_specs=(VMEM,) * 10,
        scratch_shapes=[
            pltpu.SMEM(by_offset.shape, jnp.int32),
            pltpu.SMEM(frame_index.shape, jnp.int32),
            pltpu.SemaphoreType.DMA((4,)),
        ],
        compiler_params=LIMIT,
        cost_estimate=pl.CostEstimate(flops=2 * block * width * 3 * width, bytes_accessed=4_000_000, transcendentals=0),
        name="first",
    )(
        pltpu.with_memory_space_constraint(by_offset, pltpu.HBM),
        pltpu.with_memory_space_constraint(frame_index, pltpu.HBM),
        given, activations, spatial_qkv,
    )
    kept_odd, kept_even = from_neighbours(normed)
    other_odd, other_even = from_neighbours(other)

    wide = pltpu.VMEM((rows, width), f32)
    tops_shape = pltpu.VMEM((width // PAIR, 2 * rows, PAIR), f32)
    later = (spatial_out, time_qkv, time_out)
    query, sums, tops, totals, spatial_out, time_qkv, time_out = pl.pallas_call(
        early_kernel,
        out_shape=(pltpu.VMEM((width // PAIR, 2 * rows, PAIR), bf16), wide, tops_shape, wide)
        + tuple(pltpu.VMEM(weight.shape, bf16) for weight in later),
        in_specs=[VMEM] * 8 + [HBM] * 3,
        out_specs=(VMEM,) * 7,
        scratch_shapes=[
            pltpu.VMEM((4 * block, width), bf16),
            pltpu.VMEM((width // PAIR, 4 * block, 2 * PAIR), bf16),
            pltpu.SemaphoreType.DMA((3,)),
        ],
        compiler_params=LIMIT,
        cost_estimate=pl.CostEstimate(flops=4_000_000_000, bytes_accessed=4_000_000, transcendentals=2_000_000),
        name="early",
    )(early_bias, query, keys, values, kept_odd, kept_even, other, spatial_qkv, *later)
    hidden = pl.pallas_call(
        late_kernel,
        out_shape=pltpu.VMEM((rows, width), bf16),
        in_specs=[VMEM] * 11,
        out_specs=VMEM,
        scratch_shapes=[
            pltpu.VMEM((rows, width), bf16),
            pltpu.VMEM((width // PAIR, rows, 2 * PAIR), bf16),
            pltpu.VMEM((rows, width), bf16),
        ],
        compiler_params=LIMIT,
        name="late",
    )(
        late_bias, query, sums, tops, totals, other_odd, other_even,
        base, other, spatial_qkv, spatial_out,
    )

    group = rows // members
    hidden = lax.all_to_all(hidden.reshape(members, group, width), COLUMN, 0, 0, tiled=True)

    chips = lax.axis_size("chip")
    part_of_rows = pltpu.VMEM((rows // 2, width), bf16)
    own, partner = pl.pallas_call(
        time_kernel,
        out_shape=(part_of_rows, part_of_rows),
        in_specs=[VMEM] * 5,
        out_specs=(VMEM, VMEM),
        scratch_shapes=[
            pltpu.VMEM((width // PAIR, 2 * rows, PAIR), bf16),
            pltpu.VMEM((rows, width), bf16),
            pltpu.VMEM((width // PAIR, rows, 2 * PAIR), bf16),
            pltpu.VMEM((rows, width), bf16),
            pltpu.VMEM((rows, width), bf16),
        ],
        compiler_params=LIMIT,
        name="temporal",
    )(hidden.reshape(rows, width), cosine, sine, time_qkv, time_out)
    partner = lax.ppermute(partner, "core", [(0, 1), (1, 0)])
    chunk = pltpu.VMEM((rows // chips, width), bf16)
    chunks = pl.pallas_call(
        join_kernel,
        out_shape=(chunk,) * chips,
        in_specs=[VMEM] * 2,
        out_specs=(VMEM,) * chips,
        compiler_params=SMALL,
        name="join",
    )(own, partner)
    chunks = [chunks[0]] + [
        lax.ppermute(piece, "chip", [(i, i ^ d) for i in range(chips)]) for d, piece in zip(EXCHANGES[1:], chunks[1:])
    ]
    return pl.pallas_call(
        assemble_kernel,
        out_shape=pltpu.HBM((frames_dev, block, width), bf16),
        in_specs=[VMEM] * chips,
        out_specs=HBM,
        scratch_shapes=[pltpu.SemaphoreType.DMA((2 * chips,))],
        compiler_params=SMALL,
        name="assemble",
    )(*chunks)


def solution(mesh):
    res, frame = mesh.devices.shape
    fine = Mesh(mesh.devices.reshape(res // 2, 2, frame // 2, 2), ("pair", "half", "chip", "core"))
    placed = (P(("chip", "core"), ("pair", "half"), None), P(), P(), P(), P(), P(), P())
    return jax.shard_map(
        shards, mesh=fine, in_specs=placed, out_specs=placed[0], check_vma=False
    )
```

```python
import math

import jax
import jax.numpy as jnp
from jax import lax
from jax.experimental import pallas as pl
from jax.experimental.pallas import tpu as pltpu
from jax.sharding import Mesh
from jax.sharding import PartitionSpec as P

HEAD = 64
PAIR = 2 * HEAD
EXCLUDED = -1e30
SCALE = HEAD ** (-0.5)
EXCHANGES = (0, 2, 3, 1)
COLUMN = ("half", "chip", "core")
VMEM = pl.BlockSpec(memory_space=pltpu.VMEM)
SMEM = pl.BlockSpec(memory_space=pltpu.SMEM)
HBM = pl.BlockSpec(memory_space=pltpu.HBM)
SMALL = pltpu.CompilerParams(vmem_limit_bytes=4 * 1024 * 1024)
LIMIT = pltpu.CompilerParams(vmem_limit_bytes=24 * 1024 * 1024)


def unit_rows(rows):
    widened = rows.astype(jnp.float32)
    mean_square = jnp.mean(widened * widened, axis=-1, keepdims=True)
    return (widened * lax.rsqrt(mean_square + 1e-06)).astype(jnp.bfloat16)


def dot(left, right):
    return jnp.dot(left, right, preferred_element_type=jnp.float32)


def dot_rows(left, right):
    return lax.dot_general(
        left, right, (((1,), (1,)), ((), ())), preferred_element_type=jnp.float32
    )


def by_head(pair_query):
    lane = lax.broadcasted_iota(jnp.int32, pair_query.shape, 1)
    nothing = jnp.zeros_like(pair_query)
    return jnp.concatenate(
        [jnp.where(lane < HEAD, pair_query, nothing), jnp.where(lane < HEAD, nothing, pair_query)], axis=0
    )


def side_by_side(stacked):
    rows = stacked.shape[0] // 2
    lane = lax.broadcasted_iota(jnp.int32, (rows, PAIR), 1)
    return jnp.where(lane < HEAD, stacked[:rows, :PAIR], stacked[rows:, :PAIR])


def two_rows(bias_ref, block):
    halves = [jnp.broadcast_to(bias_ref[y : y + 1, :], (block, bias_ref.shape[1])) for y in range(2)]
    return jnp.concatenate(halves * 2, axis=0)


def attend(stacked_query, keys, values, pairs, biases, finish, floors=None):
    width = keys.shape[0]

    def scores_of(pair):
        return dot_rows(stacked_query[pair], keys[:, pair * PAIR : (pair + 1) * PAIR]) + biases

    scores = scores_of(0)
    for pair in range(pairs):
        ahead = scores_of(pair + 1) if pair + 1 < pairs else None
        top = jnp.broadcast_to(jnp.max(scores, axis=-1, keepdims=True), (scores.shape[0], PAIR))
        if floors is not None:
            top = jnp.maximum(top, floors[pair])
        expo = jnp.exp(scores - jnp.concatenate([top] * (width // PAIR), axis=1)).astype(jnp.bfloat16)
        finish(pair, top, dot(expo, values[pair]))
        scores = ahead


def give_kernel(act_ref, given_ref, semaphore):
    move = pltpu.make_async_copy(act_ref.at[1 - lax.axis_index("half")], given_ref, semaphore)
    move.start()
    move.wait()


def contact_biases(contacts_ref, early_ref, late_ref):
    half, pair = lax.axis_index("half"), lax.axis_index("pair")
    block = early_ref.shape[1] // 4
    to_other = 1 - 2 * half
    odd = 4 * (pair % 2) - 2
    for row, (parity, moves) in enumerate(
        (
            (half, (0, odd, -odd, to_other, to_other + odd, to_other - odd)),
            (1 - half, (-to_other, odd - to_other, -odd - to_other, 0, odd, -odd)),
        )
    ):
        for tile, move in enumerate(moves):
            column = jnp.clip(move + 2, 0, 4)
            flag = jnp.where(column == move + 2, contacts_ref[column, 2 * pair + parity], 0)
            ref, at = (early_ref, tile) if tile < 4 else (late_ref, tile - 4)
            ref[row : row + 1, at * block : (at + 1) * block] = jnp.full(
                (1, block), jnp.where(flag > 0, 0.0, EXCLUDED), jnp.float32
            )


def rotation_tables(frame_ref, cos_ref, sin_ref):
    frames, lanes = cos_ref.shape
    row = lax.broadcasted_iota(jnp.int32, (frames, lanes), 0)
    lane = lax.broadcasted_iota(jnp.int32, (frames, lanes), 1)
    position = jnp.zeros((frames, lanes), jnp.int32)
    for j in range(frames):
        frame = 2 * (j % (frames // 2)) + j // (frames // 2)
        position = jnp.where(row == j, frame_ref[frame], position)
    half_size = HEAD // 2
    exponent = (lane % half_size).astype(jnp.float32) * (-math.log(10000.0) / half_size)
    angles = position.astype(jnp.float32) * jnp.exp(exponent)
    cos_ref[...] = jnp.cos(angles)
    sine = jnp.sin(angles)
    sin_ref[...] = jnp.where(lane % HEAD < half_size, -sine, sine)


def first_kernel(
    contacts_hbm, frame_hbm, given_ref, act_ref, qkv_hbm,
    qkv_ref, normed_ref, base_ref, query_ref, keys_ref, values_ref, early_ref, late_ref, cos_ref, sin_ref,
    contacts_ref, frame_ref, semaphores,
):
    half = lax.axis_index("half")
    width = base_ref.shape[1]
    own = pltpu.make_async_copy(act_ref.at[half], base_ref, semaphores.at[0])
    own.start()
    loads = [
        pltpu.make_async_copy(source, target, semaphores.at[at + 1])
        for at, (source, target) in enumerate(
            ((qkv_hbm, qkv_ref), (contacts_hbm, contacts_ref), (frame_hbm, frame_ref))
        )
    ]
    for load in loads:
        load.start()
    own.wait()
    normed = unit_rows(base_ref[...])
    normed_ref[...] = normed
    loads[0].wait()
    query_ref[...] = (dot(normed, qkv_ref[:, :width]) * SCALE).astype(jnp.bfloat16)
    keys_ref[...] = dot(normed, qkv_ref[:, width : 2 * width]).astype(jnp.bfloat16)
    values_ref[...] = dot(normed, qkv_ref[:, 2 * width :]).astype(jnp.bfloat16)
    for load in loads[1:]:
        load.wait()
    contact_biases(contacts_ref, early_ref, late_ref)
    rotation_tables(frame_ref, cos_ref, sin_ref)


def early_kernel(
    bias_ref, query_in, keys_in, values_in, odd_ref, even_ref, other_ref, qkv_ref, out_hbm, time_qkv_hbm,
    time_out_hbm, query_ref, sums_ref, tops_ref, totals_ref, out_ref, time_qkv_ref, time_out_ref,
    keys, values, semaphores,
):
    loads = [
        pltpu.make_async_copy(source, target, semaphores.at[at])
        for at, (source, target) in enumerate(
            ((out_hbm, out_ref), (time_qkv_hbm, time_qkv_ref), (time_out_hbm, time_out_ref))
        )
    ]
    for load in loads:
        load.start()
    block, width = other_ref.shape
    pairs = width // PAIR
    normed = unit_rows(other_ref[...])
    query = (dot(normed, qkv_ref[:, :width]) * SCALE).astype(jnp.bfloat16)
    keys[:block, :] = keys_in[...]
    tiles = jnp.concatenate([odd_ref[...], even_ref[...], normed], axis=0)
    keys[block:, :] = dot(tiles, qkv_ref[:, width : 2 * width]).astype(jnp.bfloat16)
    fresh = dot(tiles, qkv_ref[:, 2 * width :]).astype(jnp.bfloat16)
    for pair in range(pairs):
        at = slice(pair * PAIR, (pair + 1) * PAIR)
        values[pair, :block, :PAIR] = values_in[:, at]
        values[pair, block:, :PAIR] = fresh[:, at]
        values[pair, :, PAIR:] = jnp.ones((4 * block, PAIR), jnp.bfloat16)
        query_ref[pair] = by_head(jnp.concatenate([query_in[:, at], query[:, at]], axis=0))

    def finish(pair, top, product):
        at = slice(pair * PAIR, (pair + 1) * PAIR)
        tops_ref[pair] = top
        sums_ref[:, at] = side_by_side(product)
        totals_ref[:, at] = side_by_side(product[:, PAIR:])

    attend(query_ref, keys, values, pairs, two_rows(bias_ref, block), finish)
    for load in loads:
        load.wait()


def late_kernel(
    bias_ref, query_ref, sums_ref, tops_ref, totals_ref, odd_ref, even_ref,
    base_ref, other_ref, qkv_ref, out_ref, hidden_ref, keys, values, mix,
):
    half = lax.axis_index("half")
    block, width = other_ref.shape
    pairs = width // PAIR
    tiles = unit_rows(jnp.concatenate([odd_ref[...], even_ref[...]], axis=0))
    keys[...] = dot(tiles, qkv_ref[:, width : 2 * width]).astype(jnp.bfloat16)
    fresh = dot(tiles, qkv_ref[:, 2 * width :]).astype(jnp.bfloat16)
    for pair in range(pairs):
        values[pair, :, :PAIR] = fresh[:, pair * PAIR : (pair + 1) * PAIR]
        values[pair, :, PAIR:] = jnp.ones((2 * block, PAIR), jnp.bfloat16)

    def finish(pair, top, product):
        at = slice(pair * PAIR, (pair + 1) * PAIR)
        share = side_by_side(jnp.exp(tops_ref[pair] - top))
        total = totals_ref[:, at] * share + side_by_side(product[:, PAIR:])
        mix[:, at] = ((sums_ref[:, at] * share + side_by_side(product)) / total).astype(jnp.bfloat16)

    attend(query_ref, keys, values, pairs, two_rows(bias_ref, block), finish, tops_ref)
    added = dot(mix[...], out_ref[...])
    here = pl.ds(pl.multiple_of(half * block, block), block)
    there = pl.ds(pl.multiple_of((1 - half) * block, block), block)
    hidden_ref[here, :] = (base_ref[...].astype(jnp.float32) + added[:block]).astype(jnp.bfloat16)
    hidden_ref[there, :] = (other_ref[...].astype(jnp.float32) + added[block:]).astype(jnp.bfloat16)


def time_kernel(
    hidden_ref, cos_ref, sin_ref, qkv_ref, out_w_ref, own_ref, partner_ref, query, keys, values, mix, layer
):
    rows, width = hidden_ref.shape
    frames = cos_ref.shape[0]
    group = rows // frames
    normed = unit_rows(hidden_ref[...])
    cosine = jnp.concatenate(
        [jnp.broadcast_to(cos_ref[f : f + 1, :], (group, PAIR)) for f in range(frames)], axis=0
    )
    sine = jnp.concatenate(
        [jnp.broadcast_to(sin_ref[f : f + 1, :], (group, PAIR)) for f in range(frames)], axis=0
    )
    source = lax.broadcasted_iota(jnp.int32, (PAIR, PAIR), 0)
    target = lax.broadcasted_iota(jnp.int32, (PAIR, PAIR), 1)
    exchange = jnp.where(source == target ^ (HEAD // 2), 1.0, 0.0).astype(jnp.bfloat16)

    def rotate(entries):
        entries = entries.astype(jnp.bfloat16)
        return entries.astype(jnp.float32) * cosine + dot(entries, exchange) * sine

    pairs = width // PAIR
    projected = dot(normed, qkv_ref[...])
    for pair in range(pairs):
        at = slice(pair * PAIR, (pair + 1) * PAIR)
        query[pair] = by_head((rotate(projected[:, at]) * SCALE).astype(jnp.bfloat16))
        keys[:, at] = rotate(projected[:, width + pair * PAIR : width + (pair + 1) * PAIR]).astype(jnp.bfloat16)
        values[pair, :, :PAIR] = projected[:, 2 * width + pair * PAIR : 2 * width + (pair + 1) * PAIR].astype(jnp.bfloat16)
        values[pair, :, PAIR:] = jnp.ones((rows, PAIR), jnp.bfloat16)
    row = lax.broadcasted_iota(jnp.int32, (2 * rows, rows), 0)
    column = lax.broadcasted_iota(jnp.int32, (2 * rows, rows), 1)
    biases = jnp.where(row % group == column % group, 0.0, EXCLUDED)

    def finish(pair, top, product):
        mixed = side_by_side(product) / side_by_side(product[:, PAIR:])
        mix[:, pair * PAIR : (pair + 1) * PAIR] = mixed.astype(jnp.bfloat16)

    attend(query, keys, values, pairs, biases, finish)
    added = (hidden_ref[...].astype(jnp.float32) + dot(mix[...], out_w_ref[...])).astype(jnp.bfloat16)
    per_half = frames // 2
    for j in range(frames):
        target = (j % 2) * per_half + (j % per_half) // 2 * 2 + j // per_half
        layer[target * group : (target + 1) * group, :] = added[j * group : (j + 1) * group, :]
    core = lax.axis_index("core")
    own_ref[...] = layer[pl.ds(pl.multiple_of(core * (rows // 2), rows // 2), rows // 2), :]
    partner_ref[...] = layer[pl.ds(pl.multiple_of((1 - core) * (rows // 2), rows // 2), rows // 2), :]


def join_kernel(own_ref, partner_ref, *chunk_refs):
    chip, core = lax.axis_index("chip"), lax.axis_index("core")
    rows = own_ref.shape[0] // len(chunk_refs)
    group = rows // 2
    for d, chunk_ref in zip(EXCHANGES, chunk_refs):
        for frame in range(2):
            at = pl.ds(pl.multiple_of((chip ^ d) * rows + frame * group, group), group)
            here = pl.ds(pl.multiple_of(frame * rows + core * group, group), group)
            there = pl.ds(pl.multiple_of(frame * rows + (1 - core) * group, group), group)
            chunk_ref[here, :] = own_ref[at, :]
            chunk_ref[there, :] = partner_ref[at, :]


def assemble_kernel(*refs):
    *chunk_refs, layer_ref, semaphores = refs
    chip = lax.axis_index("chip")
    rows = chunk_refs[0].shape[0] // 2
    moves = []
    for d, chunk_ref in zip(EXCHANGES, chunk_refs):
        at = pl.ds(pl.multiple_of((chip ^ d) * rows, rows), rows)
        for frame in range(2):
            moves.append(
                pltpu.make_async_copy(
                    chunk_ref.at[pl.ds(frame * rows, rows), :], layer_ref.at[frame, at, :], semaphores.at[2 * d + frame]
                )
            )
            moves[-1].start()
    for move in moves:
        move.wait()


def shards(activations, contacts, frame_index, spatial_qkv, spatial_out, time_qkv, time_out):
    frames_dev, block, width = activations.shape
    pairs = lax.axis_size("pair")
    activations, spatial_qkv, spatial_out, time_qkv, time_out = (
        pltpu.with_memory_space_constraint(x, pltpu.HBM)
        for x in (activations, spatial_qkv, spatial_out, time_qkv, time_out)
    )
    rows = 2 * block
    bf16, f32 = jnp.bfloat16, jnp.float32
    given = pl.pallas_call(
        give_kernel,
        out_shape=pltpu.VMEM((block, width), bf16),
        in_specs=[HBM],
        out_specs=VMEM,
        scratch_shapes=[pltpu.SemaphoreType.DMA],
        name="give",
    )(activations)
    other = lax.ppermute(given, "half", [(0, 1), (1, 0)])

    column = lax.axis_size("half") * lax.axis_size("chip") * lax.axis_size("core")
    even, odd = [], []
    for i in range(pairs):
        for place in range(column):
            at = i * column + place
            even.append((at, (i ^ 1) * column + place))
            if i in (0, pairs - 1):
                odd.append((at, at ^ 1))
            else:
                odd.append((at, (((i - 1) ^ 1) + 1) * column + place))

    def from_neighbours(tile):
        axes = ("pair",) + COLUMN
        return lax.ppermute(tile, axes, odd), lax.ppermute(tile, axes, even)

    tile_in_vmem = pltpu.VMEM((block, width), bf16)
    members = 2 * lax.axis_size("chip") * lax.axis_size("core")
    table = pltpu.VMEM((members, PAIR), f32)
    by_offset = contacts.T
    spatial_qkv, normed, base, query, keys, values, early_bias, late_bias, cosine, sine = pl.pallas_call(
        first_kernel,
        out_shape=(pltpu.VMEM(spatial_qkv.shape, bf16),)
        + (tile_in_vmem,) * 5
        + (pltpu.VMEM((2, 4 * block), f32), pltpu.VMEM((2, 2 * block), f32), table, table),
        in_specs=[HBM] * 2 + [VMEM] + [HBM] * 2,
        out_specs=(VMEM,) * 10,
        scratch_shapes=[
            pltpu.SMEM(by_offset.shape, jnp.int32),
            pltpu.SMEM(frame_index.shape, jnp.int32),
            pltpu.SemaphoreType.DMA((4,)),
        ],
        compiler_params=LIMIT,
        cost_estimate=pl.CostEstimate(flops=2 * block * width * 3 * width, bytes_accessed=4_000_000, transcendentals=0),
        name="first",
    )(
        pltpu.with_memory_space_constraint(by_offset, pltpu.HBM),
        pltpu.with_memory_space_constraint(frame_index, pltpu.HBM),
        given, activations, spatial_qkv,
    )
    kept_odd, kept_even = from_neighbours(normed)
    other_odd, other_even = from_neighbours(other)

    wide = pltpu.VMEM((rows, width), f32)
    tops_shape = pltpu.VMEM((width // PAIR, 2 * rows, PAIR), f32)
    later = (spatial_out, time_qkv, time_out)
    query, sums, tops, totals, spatial_out, time_qkv, time_out = pl.pallas_call(
        early_kernel,
        out_shape=(pltpu.VMEM((width // PAIR, 2 * rows, PAIR), bf16), wide, tops_shape, wide)
        + tuple(pltpu.VMEM(weight.shape, bf16) for weight in later),
        in_specs=[VMEM] * 8 + [HBM] * 3,
        out_specs=(VMEM,) * 7,
        scratch_shapes=[
            pltpu.VMEM((4 * block, width), bf16),
            pltpu.VMEM((width // PAIR, 4 * block, 2 * PAIR), bf16),
            pltpu.SemaphoreType.DMA((3,)),
        ],
        compiler_params=LIMIT,
        cost_estimate=pl.CostEstimate(flops=4_000_000_000, bytes_accessed=4_000_000, transcendentals=2_000_000),
        name="early",
    )(early_bias, query, keys, values, kept_odd, kept_even, other, spatial_qkv, *later)
    hidden = pl.pallas_call(
        late_kernel,
        out_shape=pltpu.VMEM((rows, width), bf16),
        in_specs=[VMEM] * 11,
        out_specs=VMEM,
        scratch_shapes=[
            pltpu.VMEM((rows, width), bf16),
            pltpu.VMEM((width // PAIR, rows, 2 * PAIR), bf16),
            pltpu.VMEM((rows, width), bf16),
        ],
        compiler_params=LIMIT,
        name="late",
    )(
        late_bias, query, sums, tops, totals, other_odd, other_even,
        base, other, spatial_qkv, spatial_out,
    )

    group = rows // members
    hidden = lax.all_to_all(hidden.reshape(members, group, width), COLUMN, 0, 0, tiled=True)

    chips = lax.axis_size("chip")
    part_of_rows = pltpu.VMEM((rows // 2, width), bf16)
    own, partner = pl.pallas_call(
        time_kernel,
        out_shape=(part_of_rows, part_of_rows),
        in_specs=[VMEM] * 5,
        out_specs=(VMEM, VMEM),
        scratch_shapes=[
            pltpu.VMEM((width // PAIR, 2 * rows, PAIR), bf16),
            pltpu.VMEM((rows, width), bf16),
            pltpu.VMEM((width // PAIR, rows, 2 * PAIR), bf16),
            pltpu.VMEM((rows, width), bf16),
            pltpu.VMEM((rows, width), bf16),
        ],
        compiler_params=LIMIT,
        name="temporal",
    )(hidden.reshape(rows, width), cosine, sine, time_qkv, time_out)
    partner = lax.ppermute(partner, "core", [(0, 1), (1, 0)])
    chunk = pltpu.VMEM((rows // chips, width), bf16)
    chunks = pl.pallas_call(
        join_kernel,
        out_shape=(chunk,) * chips,
        in_specs=[VMEM] * 2,
        out_specs=(VMEM,) * chips,
        compiler_params=SMALL,
        name="join",
    )(own, partner)
    chunks = [chunks[0]] + [
        lax.ppermute(piece, "chip", [(i, i ^ d) for i in range(chips)]) for d, piece in zip(EXCHANGES[1:], chunks[1:])
    ]
    return pl.pallas_call(
        assemble_kernel,
        out_shape=pltpu.HBM((frames_dev, block, width), bf16),
        in_specs=[VMEM] * chips,
        out_specs=HBM,
        scratch_shapes=[pltpu.SemaphoreType.DMA((2 * chips,))],
        compiler_params=SMALL,
        name="assemble",
    )(*chunks)


def solution(mesh):
    res, frame = mesh.devices.shape
    fine = Mesh(mesh.devices.reshape(res // 2, 2, frame // 2, 2), ("pair", "half", "chip", "core"))
    placed = (P(("chip", "core"), ("pair", "half"), None), P(), P(), P(), P(), P(), P())
    return jax.shard_map(
        shards, mesh=fine, in_specs=placed, out_specs=placed[0], check_vma=False
    )
```

```python
import math

import jax
import jax.numpy as jnp
from jax import lax
from jax.experimental import pallas as pl
from jax.experimental.pallas import tpu as pltpu
from jax.sharding import Mesh
from jax.sharding import PartitionSpec as P

HEAD = 64
PAIR = 2 * HEAD
EXCLUDED = -1e30
SCALE = HEAD ** (-0.5)
EXCHANGES = (0, 2, 3, 1)
COLUMN = ("half", "chip", "core")
VMEM = pl.BlockSpec(memory_space=pltpu.VMEM)
SMEM = pl.BlockSpec(memory_space=pltpu.SMEM)
HBM = pl.BlockSpec(memory_space=pltpu.HBM)
SMALL = pltpu.CompilerParams(vmem_limit_bytes=4 * 1024 * 1024)
LIMIT = pltpu.CompilerParams(vmem_limit_bytes=24 * 1024 * 1024)


def row_scale(rows):
    widened = rows.astype(jnp.float32)
    return lax.rsqrt(jnp.mean(widened * widened, axis=-1, keepdims=True) + 1e-06)


def unit_rows(rows):
    widened = rows.astype(jnp.float32)
    mean_square = jnp.mean(widened * widened, axis=-1, keepdims=True)
    return (widened * lax.rsqrt(mean_square + 1e-06)).astype(jnp.bfloat16)


def dot(left, right):
    return jnp.dot(left, right, preferred_element_type=jnp.float32)


def dot_rows(left, right):
    return lax.dot_general(
        left, right, (((1,), (1,)), ((), ())), preferred_element_type=jnp.float32
    )


def by_head(pair_query):
    lane = lax.broadcasted_iota(jnp.int32, pair_query.shape, 1)
    nothing = jnp.zeros_like(pair_query)
    return jnp.concatenate(
        [jnp.where(lane < HEAD, pair_query, nothing), jnp.where(lane < HEAD, nothing, pair_query)], axis=0
    )


def side_by_side(stacked):
    rows = stacked.shape[0] // 2
    lane = lax.broadcasted_iota(jnp.int32, (rows, PAIR), 1)
    return jnp.where(lane < HEAD, stacked[:rows, :PAIR], stacked[rows:, :PAIR])


def two_rows(bias_ref, block):
    halves = [jnp.broadcast_to(bias_ref[y : y + 1, :], (block, bias_ref.shape[1])) for y in range(2)]
    return jnp.concatenate(halves * 2, axis=0)


def attend(stacked_query, keys, values, pairs, biases, finish, floors=None):
    width = keys.shape[0]

    def scores_of(pair):
        return dot_rows(stacked_query[pair], keys[:, pair * PAIR : (pair + 1) * PAIR]) + biases

    scores = scores_of(0)
    for pair in range(pairs):
        ahead = scores_of(pair + 1) if pair + 1 < pairs else None
        top = jnp.broadcast_to(jnp.max(scores, axis=-1, keepdims=True), (scores.shape[0], PAIR))
        if floors is not None:
            top = jnp.maximum(top, floors[pair])
        expo = jnp.exp(scores - jnp.concatenate([top] * (width // PAIR), axis=1)).astype(jnp.bfloat16)
        finish(pair, top, dot(expo, values[pair]))
        scores = ahead


def give_kernel(act_ref, given_ref, semaphore):
    move = pltpu.make_async_copy(act_ref.at[1 - lax.axis_index("half")], given_ref, semaphore)
    move.start()
    move.wait()


def contact_biases(contacts_ref, early_ref, late_ref):
    half, pair = lax.axis_index("half"), lax.axis_index("pair")
    block = early_ref.shape[1] // 4
    to_other = 1 - 2 * half
    odd = 4 * (pair % 2) - 2
    for row, (parity, moves) in enumerate(
        (
            (half, (0, odd, -odd, to_other, to_other + odd, to_other - odd)),
            (1 - half, (-to_other, odd - to_other, -odd - to_other, 0, odd, -odd)),
        )
    ):
        for tile, move in enumerate(moves):
            column = jnp.clip(move + 2, 0, 4)
            flag = jnp.where(column == move + 2, contacts_ref[column, 2 * pair + parity], 0)
            ref, at = (early_ref, tile) if tile < 4 else (late_ref, tile - 4)
            ref[row : row + 1, at * block : (at + 1) * block] = jnp.full(
                (1, block), jnp.where(flag > 0, 0.0, EXCLUDED), jnp.float32
            )


def rotation_tables(frame_ref, cos_ref, sin_ref):
    frames, lanes = cos_ref.shape
    row = lax.broadcasted_iota(jnp.int32, (frames, lanes), 0)
    lane = lax.broadcasted_iota(jnp.int32, (frames, lanes), 1)
    position = jnp.zeros((frames, lanes), jnp.int32)
    for j in range(frames):
        frame = 2 * (j % (frames // 2)) + j // (frames // 2)
        position = jnp.where(row == j, frame_ref[frame], position)
    half_size = HEAD // 2
    exponent = (lane % half_size).astype(jnp.float32) * (-math.log(10000.0) / half_size)
    angles = position.astype(jnp.float32) * jnp.exp(exponent)
    cos_ref[...] = jnp.cos(angles)
    sine = jnp.sin(angles)
    sin_ref[...] = jnp.where(lane % HEAD < half_size, -sine, sine)


def first_kernel(
    contacts_hbm, frame_hbm, given_ref, act_ref, qkv_hbm,
    qkv_ref, normed_ref, base_ref, query_ref, keys_ref, values_ref, early_ref, late_ref, cos_ref, sin_ref,
    contacts_ref, frame_ref, semaphores,
):
    half = lax.axis_index("half")
    width = base_ref.shape[1]
    own = pltpu.make_async_copy(act_ref.at[half], base_ref, semaphores.at[0])
    own.start()
    loads = [
        pltpu.make_async_copy(source, target, semaphores.at[at + 1])
        for at, (source, target) in enumerate(
            ((qkv_hbm, qkv_ref), (contacts_hbm, contacts_ref), (frame_hbm, frame_ref))
        )
    ]
    for load in loads:
        load.start()
    own.wait()
    normed = unit_rows(base_ref[...])
    normed_ref[...] = normed
    loads[0].wait()
    query_ref[...] = (dot(normed, qkv_ref[:, :width]) * SCALE).astype(jnp.bfloat16)
    keys_ref[...] = dot(normed, qkv_ref[:, width : 2 * width]).astype(jnp.bfloat16)
    values_ref[...] = dot(normed, qkv_ref[:, 2 * width :]).astype(jnp.bfloat16)
    for load in loads[1:]:
        load.wait()
    contact_biases(contacts_ref, early_ref, late_ref)
    rotation_tables(frame_ref, cos_ref, sin_ref)


def early_kernel(
    bias_ref, query_in, keys_in, values_in, odd_ref, even_ref, other_ref, qkv_ref, out_hbm, time_qkv_hbm,
    time_out_hbm, query_ref, sums_ref, tops_ref, totals_ref, out_ref, time_qkv_ref, time_out_ref,
    keys, values, semaphores,
):
    loads = [
        pltpu.make_async_copy(source, target, semaphores.at[at])
        for at, (source, target) in enumerate(
            ((out_hbm, out_ref), (time_qkv_hbm, time_qkv_ref), (time_out_hbm, time_out_ref))
        )
    ]
    for load in loads:
        load.start()
    block, width = other_ref.shape
    pairs = width // PAIR
    normed = unit_rows(other_ref[...])
    query = (dot(normed, qkv_ref[:, :width]) * SCALE).astype(jnp.bfloat16)
    keys[:block, :] = keys_in[...]
    tiles = jnp.concatenate([odd_ref[...], even_ref[...], normed], axis=0)
    keys[block:, :] = dot(tiles, qkv_ref[:, width : 2 * width]).astype(jnp.bfloat16)
    fresh = dot(tiles, qkv_ref[:, 2 * width :]).astype(jnp.bfloat16)
    for pair in range(pairs):
        at = slice(pair * PAIR, (pair + 1) * PAIR)
        values[pair, :block, :PAIR] = values_in[:, at]
        values[pair, block:, :PAIR] = fresh[:, at]
        values[pair, :, PAIR:] = jnp.ones((4 * block, PAIR), jnp.bfloat16)
        query_ref[pair] = by_head(jnp.concatenate([query_in[:, at], query[:, at]], axis=0))

    def finish(pair, top, product):
        at = slice(pair * PAIR, (pair + 1) * PAIR)
        tops_ref[pair] = top
        sums_ref[:, at] = side_by_side(product)
        totals_ref[:, at] = side_by_side(product[:, PAIR:])

    attend(query_ref, keys, values, pairs, two_rows(bias_ref, block), finish)
    for load in loads:
        load.wait()


def late_kernel(
    bias_ref, query_ref, sums_ref, tops_ref, totals_ref, odd_ref, even_ref,
    base_ref, other_ref, qkv_ref, out_ref, hidden_ref, keys, values, mix,
):
    half = lax.axis_index("half")
    block, width = other_ref.shape
    pairs = width // PAIR
    tiles = jnp.concatenate([odd_ref[...], even_ref[...]], axis=0)
    scale = row_scale(tiles)
    keys[...] = (dot(tiles, qkv_ref[:, width : 2 * width]) * scale).astype(jnp.bfloat16)
    fresh = (dot(tiles, qkv_ref[:, 2 * width :]) * scale).astype(jnp.bfloat16)
    for pair in range(pairs):
        values[pair, :, :PAIR] = fresh[:, pair * PAIR : (pair + 1) * PAIR]
        values[pair, :, PAIR:] = jnp.ones((2 * block, PAIR), jnp.bfloat16)

    def finish(pair, top, product):
        at = slice(pair * PAIR, (pair + 1) * PAIR)
        share = side_by_side(jnp.exp(tops_ref[pair] - top))
        total = totals_ref[:, at] * share + side_by_side(product[:, PAIR:])
        mix[:, at] = ((sums_ref[:, at] * share + side_by_side(product)) / total).astype(jnp.bfloat16)

    attend(query_ref, keys, values, pairs, two_rows(bias_ref, block), finish, tops_ref)
    added = dot(mix[...], out_ref[...])
    here = pl.ds(pl.multiple_of(half * block, block), block)
    there = pl.ds(pl.multiple_of((1 - half) * block, block), block)
    hidden_ref[here, :] = (base_ref[...].astype(jnp.float32) + added[:block]).astype(jnp.bfloat16)
    hidden_ref[there, :] = (other_ref[...].astype(jnp.float32) + added[block:]).astype(jnp.bfloat16)


def time_kernel(
    hidden_ref, cos_ref, sin_ref, qkv_ref, out_w_ref, own_ref, partner_ref, query, keys, values, mix, layer
):
    rows, width = hidden_ref.shape
    frames = cos_ref.shape[0]
    group = rows // frames
    hidden = hidden_ref[...]
    cosine = jnp.concatenate(
        [jnp.broadcast_to(cos_ref[f : f + 1, :], (group, PAIR)) for f in range(frames)], axis=0
    )
    sine = jnp.concatenate(
        [jnp.broadcast_to(sin_ref[f : f + 1, :], (group, PAIR)) for f in range(frames)], axis=0
    )
    source = lax.broadcasted_iota(jnp.int32, (PAIR, PAIR), 0)
    target = lax.broadcasted_iota(jnp.int32, (PAIR, PAIR), 1)
    exchange = jnp.where(source == target ^ (HEAD // 2), 1.0, 0.0).astype(jnp.bfloat16)

    def rotate(entries):
        entries = entries.astype(jnp.bfloat16)
        return entries.astype(jnp.float32) * cosine + dot(entries, exchange) * sine

    pairs = width // PAIR
    projected = dot(hidden, qkv_ref[...]) * row_scale(hidden)
    for pair in range(pairs):
        at = slice(pair * PAIR, (pair + 1) * PAIR)
        query[pair] = by_head((rotate(projected[:, at]) * SCALE).astype(jnp.bfloat16))
        keys[:, at] = rotate(projected[:, width + pair * PAIR : width + (pair + 1) * PAIR]).astype(jnp.bfloat16)
        values[pair, :, :PAIR] = projected[:, 2 * width + pair * PAIR : 2 * width + (pair + 1) * PAIR].astype(jnp.bfloat16)
        values[pair, :, PAIR:] = jnp.ones((rows, PAIR), jnp.bfloat16)
    row = lax.broadcasted_iota(jnp.int32, (2 * rows, rows), 0)
    column = lax.broadcasted_iota(jnp.int32, (2 * rows, rows), 1)
    biases = jnp.where(row % group == column % group, 0.0, EXCLUDED)

    def finish(pair, top, product):
        mixed = side_by_side(product) / side_by_side(product[:, PAIR:])
        mix[:, pair * PAIR : (pair + 1) * PAIR] = mixed.astype(jnp.bfloat16)

    attend(query, keys, values, pairs, biases, finish)
    added = (hidden_ref[...].astype(jnp.float32) + dot(mix[...], out_w_ref[...])).astype(jnp.bfloat16)
    per_half = frames // 2
    for j in range(frames):
        target = (j % 2) * per_half + (j % per_half) // 2 * 2 + j // per_half
        layer[target * group : (target + 1) * group, :] = added[j * group : (j + 1) * group, :]
    core = lax.axis_index("core")
    own_ref[...] = layer[pl.ds(pl.multiple_of(core * (rows // 2), rows // 2), rows // 2), :]
    partner_ref[...] = layer[pl.ds(pl.multiple_of((1 - core) * (rows // 2), rows // 2), rows // 2), :]


def join_kernel(own_ref, partner_ref, *chunk_refs):
    chip, core = lax.axis_index("chip"), lax.axis_index("core")
    rows = own_ref.shape[0] // len(chunk_refs)
    group = rows // 2
    for d, chunk_ref in zip(EXCHANGES, chunk_refs):
        for frame in range(2):
            at = pl.ds(pl.multiple_of((chip ^ d) * rows + frame * group, group), group)
            here = pl.ds(pl.multiple_of(frame * rows + core * group, group), group)
            there = pl.ds(pl.multiple_of(frame * rows + (1 - core) * group, group), group)
            chunk_ref[here, :] = own_ref[at, :]
            chunk_ref[there, :] = partner_ref[at, :]


def assemble_kernel(*refs):
    *chunk_refs, layer_ref, semaphores = refs
    chip = lax.axis_index("chip")
    rows = chunk_refs[0].shape[0] // 2
    moves = []
    for d, chunk_ref in zip(EXCHANGES, chunk_refs):
        at = pl.ds(pl.multiple_of((chip ^ d) * rows, rows), rows)
        for frame in range(2):
            moves.append(
                pltpu.make_async_copy(
                    chunk_ref.at[pl.ds(frame * rows, rows), :], layer_ref.at[frame, at, :], semaphores.at[2 * d + frame]
                )
            )
            moves[-1].start()
    for move in moves:
        move.wait()


def shards(activations, contacts, frame_index, spatial_qkv, spatial_out, time_qkv, time_out):
    frames_dev, block, width = activations.shape
    pairs = lax.axis_size("pair")
    activations, spatial_qkv, spatial_out, time_qkv, time_out = (
        pltpu.with_memory_space_constraint(x, pltpu.HBM)
        for x in (activations, spatial_qkv, spatial_out, time_qkv, time_out)
    )
    rows = 2 * block
    bf16, f32 = jnp.bfloat16, jnp.float32
    given = pl.pallas_call(
        give_kernel,
        out_shape=pltpu.VMEM((block, width), bf16),
        in_specs=[HBM],
        out_specs=VMEM,
        scratch_shapes=[pltpu.SemaphoreType.DMA],
        name="give",
    )(activations)
    other = lax.ppermute(given, "half", [(0, 1), (1, 0)])

    column = lax.axis_size("half") * lax.axis_size("chip") * lax.axis_size("core")
    even, odd = [], []
    for i in range(pairs):
        for place in range(column):
            at = i * column + place
            even.append((at, (i ^ 1) * column + place))
            if i in (0, pairs - 1):
                odd.append((at, at ^ 1))
            else:
                odd.append((at, (((i - 1) ^ 1) + 1) * column + place))

    def from_neighbours(tile):
        axes = ("pair",) + COLUMN
        return lax.ppermute(tile, axes, odd), lax.ppermute(tile, axes, even)

    tile_in_vmem = pltpu.VMEM((block, width), bf16)
    members = 2 * lax.axis_size("chip") * lax.axis_size("core")
    table = pltpu.VMEM((members, PAIR), f32)
    by_offset = contacts.T
    spatial_qkv, normed, base, query, keys, values, early_bias, late_bias, cosine, sine = pl.pallas_call(
        first_kernel,
        out_shape=(pltpu.VMEM(spatial_qkv.shape, bf16),)
        + (tile_in_vmem,) * 5
        + (pltpu.VMEM((2, 4 * block), f32), pltpu.VMEM((2, 2 * block), f32), table, table),
        in_specs=[HBM] * 2 + [VMEM] + [HBM] * 2,
        out_specs=(VMEM,) * 10,
        scratch_shapes=[
            pltpu.SMEM(by_offset.shape, jnp.int32),
            pltpu.SMEM(frame_index.shape, jnp.int32),
            pltpu.SemaphoreType.DMA((4,)),
        ],
        compiler_params=LIMIT,
        cost_estimate=pl.CostEstimate(flops=2 * block * width * 3 * width, bytes_accessed=4_000_000, transcendentals=0),
        name="first",
    )(
        pltpu.with_memory_space_constraint(by_offset, pltpu.HBM),
        pltpu.with_memory_space_constraint(frame_index, pltpu.HBM),
        given, activations, spatial_qkv,
    )
    kept_odd, kept_even = from_neighbours(normed)
    other_odd, other_even = from_neighbours(other)

    wide = pltpu.VMEM((rows, width), f32)
    tops_shape = pltpu.VMEM((width // PAIR, 2 * rows, PAIR), f32)
    later = (spatial_out, time_qkv, time_out)
    query, sums, tops, totals, spatial_out, time_qkv, time_out = pl.pallas_call(
        early_kernel,
        out_shape=(pltpu.VMEM((width // PAIR, 2 * rows, PAIR), bf16), wide, tops_shape, wide)
        + tuple(pltpu.VMEM(weight.shape, bf16) for weight in later),
        in_specs=[VMEM] * 8 + [HBM] * 3,
        out_specs=(VMEM,) * 7,
        scratch_shapes=[
            pltpu.VMEM((4 * block, width), bf16),
            pltpu.VMEM((width // PAIR, 4 * block, 2 * PAIR), bf16),
            pltpu.SemaphoreType.DMA((3,)),
        ],
        compiler_params=LIMIT,
        cost_estimate=pl.CostEstimate(flops=4_000_000_000, bytes_accessed=4_000_000, transcendentals=2_000_000),
        name="early",
    )(early_bias, query, keys, values, kept_odd, kept_even, other, spatial_qkv, *later)
    hidden = pl.pallas_call(
        late_kernel,
        out_shape=pltpu.VMEM((rows, width), bf16),
        in_specs=[VMEM] * 11,
        out_specs=VMEM,
        scratch_shapes=[
            pltpu.VMEM((rows, width), bf16),
            pltpu.VMEM((width // PAIR, rows, 2 * PAIR), bf16),
            pltpu.VMEM((rows, width), bf16),
        ],
        compiler_params=LIMIT,
        name="late",
    )(
        late_bias, query, sums, tops, totals, other_odd, other_even,
        base, other, spatial_qkv, spatial_out,
    )

    group = rows // members
    hidden = lax.all_to_all(hidden.reshape(members, group, width), COLUMN, 0, 0, tiled=True)

    chips = lax.axis_size("chip")
    part_of_rows = pltpu.VMEM((rows // 2, width), bf16)
    own, partner = pl.pallas_call(
        time_kernel,
        out_shape=(part_of_rows, part_of_rows),
        in_specs=[VMEM] * 5,
        out_specs=(VMEM, VMEM),
        scratch_shapes=[
            pltpu.VMEM((width // PAIR, 2 * rows, PAIR), bf16),
            pltpu.VMEM((rows, width), bf16),
            pltpu.VMEM((width // PAIR, rows, 2 * PAIR), bf16),
            pltpu.VMEM((rows, width), bf16),
            pltpu.VMEM((rows, width), bf16),
        ],
        compiler_params=LIMIT,
        name="temporal",
    )(hidden.reshape(rows, width), cosine, sine, time_qkv, time_out)
    partner = lax.ppermute(partner, "core", [(0, 1), (1, 0)])
    chunk = pltpu.VMEM((rows // chips, width), bf16)
    chunks = pl.pallas_call(
        join_kernel,
        out_shape=(chunk,) * chips,
        in_specs=[VMEM] * 2,
        out_specs=(VMEM,) * chips,
        compiler_params=SMALL,
        name="join",
    )(own, partner)
    chunks = [chunks[0]] + [
        lax.ppermute(piece, "chip", [(i, i ^ d) for i in range(chips)]) for d, piece in zip(EXCHANGES[1:], chunks[1:])
    ]
    return pl.pallas_call(
        assemble_kernel,
        out_shape=pltpu.HBM((frames_dev, block, width), bf16),
        in_specs=[VMEM] * chips,
        out_specs=HBM,
        scratch_shapes=[pltpu.SemaphoreType.DMA((2 * chips,))],
        compiler_params=SMALL,
        name="assemble",
    )(*chunks)


def solution(mesh):
    res, frame = mesh.devices.shape
    fine = Mesh(mesh.devices.reshape(res // 2, 2, frame // 2, 2), ("pair", "half", "chip", "core"))
    placed = (P(("chip", "core"), ("pair", "half"), None), P(), P(), P(), P(), P(), P())
    return jax.shard_map(
        shards, mesh=fine, in_specs=placed, out_specs=placed[0], check_vma=False
    )
```
